512 devices in a mesh: grp: 16 (over y, x_lo), blk: 32 (over z, x_hi, core).
Axes of the slice: x: 4 (x_hi: 2, x_lo: 2; x = x_hi * 2 + x_lo), y: 8, z: 8, core: 2. Of those that a mesh axis runs over, the one named last changes fastest.
Arguments:
- tile_values: bfloat16 [512, 6, 256, 256], P(('grp', 'blk')), may hold values from 0.019897461 to 1
- tile_offset: int32 [512, 6], P(('grp', 'blk')), may hold values from 0 to 7, as said below
- tile_exponent: int32 [512, 6], P(('grp', 'blk')), may hold values from -2 to 2
- initial_vectors: bfloat16 [131072, 64], P(('grp', 'blk')), may hold values from -6 to 6
Outputs:
- spectral_vectors: float32 [131072, 64], P(('grp', 'blk'))
The draws below stay inside these ranges and needn't reach their ends.
Inputs may be any that keep to these rules, and one draw needn't show every extreme that they name: `tile_offset`: in each row slot 0 holds 0 and the offsets are distinct and ascending.
All inputs are finite; a program needn't handle non-finite values.
Results may differ from the reference program's by a relative error of at most 0.0041.
Values may be sent and summed in bfloat16 or wider, within the bound.
A program may use at most 64 MiB of HBM per device.

```python
import math
import jax
import jax.numpy as jnp
from jax import lax

TILE = 256
VEC = 64
SPAN = 8
SLOTS = 6
NB = 512
NODES = 131072
N_BLK = 32


def draw_tile_offset(key, part):
    key = jax.random.fold_in(key, 7)
    scores = jax.random.randint(key, (NB, SPAN - 1), 0, 1000) * SPAN + jnp.arange(SPAN - 1)[None, :]
    scores = scores.at[0, SPAN - 2].set(1000 * SPAN + SPAN)
    ignored, picked = lax.top_k(scores, SLOTS - 1)
    others = jnp.sort(picked + 1, axis=1)
    return jnp.concatenate([jnp.zeros((NB, 1), jnp.int32), others.astype(jnp.int32)], axis=1).astype(jnp.int32)


def place_ends(array, key, low, high):
    longest = array.shape.index(max(array.shape))
    spots = []
    for shift in (0, 1):
        where = [jax.random.randint(jax.random.fold_in(key, axis), (), 0, length) for axis, length in enumerate(array.shape)]
        where[longest] = (where[longest] + shift) % array.shape[longest]
        spots.append(tuple(where))
    return array.at[spots[0]].set(low).at[spots[1]].set(high)


def level_of(own_key, shape, cuts, low, largest):
    loudness = 1.0
    for dim, blocks in cuts:
        draws = jax.random.uniform(jax.random.fold_in(jax.random.fold_in(own_key, 6), dim), (blocks,), jnp.float32, low / len(cuts), largest / len(cuts))
        loudness = loudness * jnp.repeat(jnp.exp(draws), shape[dim] // blocks).reshape((-1,) + (1,) * (len(shape) - 1 - dim))
    return loudness


def noise(own_key, dims, width, bound, shards=(), kind=jnp.bfloat16):
    loudness = level_of(own_key, dims, shards, -0.22, 0.18) if shards else 1.0
    drawn = jax.random.normal(own_key, dims, jnp.float32) * width * loudness
    return jnp.minimum(jnp.maximum(drawn, -bound), bound).astype(kind)


def setup_inputs(seed: int = 0) -> dict:
    seeds = jax.random.split(jax.random.key(seed), 5)
    tile_values = jnp.clip(jnp.exp(math.log(1.0) - 3.9171631 * jax.random.uniform(seeds[0], (NB, SLOTS, TILE, TILE), jnp.float32) ** level_of(seeds[0], (NB, SLOTS, TILE, TILE), ((0, 512),), -0.2, 0.2)), 0.019897461, 1.0).astype(jnp.bfloat16)
    tile_offset = draw_tile_offset(jax.random.fold_in(seeds[4], 71), 0)
    tile_exponent = place_ends(jax.random.randint(seeds[2], (NB, SLOTS), -2, 3), jax.random.fold_in(seeds[2], 1), -2, 2).astype(jnp.int32)
    initial_vectors = noise(seeds[3], (NODES, VEC), 1.0, 6.0, ((0, 512),))
    return {"tile_values": tile_values, "tile_offset": tile_offset, "tile_exponent": tile_exponent, "initial_vectors": initial_vectors}


def power_of_two(exponent):
    return jnp.where(exponent == -2, 0.25, jnp.where(exponent == -1, 0.5, jnp.where(exponent == 0, 1.0, jnp.where(exponent == 1, 2.0, 4.0)))).astype(jnp.float32)

def orthonormal(image):
    gram_matrix = jnp.dot(image.T.astype(jnp.float32), image.astype(jnp.float32), precision=lax.Precision.HIGHEST, preferred_element_type=jnp.float32) / NODES
    factor_lower = jnp.linalg.cholesky(gram_matrix)
    return jax.scipy.linalg.solve_triangular(factor_lower, image.T, lower=True).T

def reference(tile_values, tile_offset, tile_exponent, initial_vectors):
    row_ids = jnp.arange(NB, dtype=jnp.int32)
    group_base = row_ids // N_BLK * N_BLK
    columns = (group_base[:, None] + (row_ids[:, None] % N_BLK + tile_offset) % N_BLK).astype(jnp.int32)
    scale = power_of_two(tile_exponent)

    def scaled_tile(row, slot):
        return (tile_values[row, slot].astype(jnp.float32) * scale[row, slot]).astype(jnp.bfloat16)

    def motif_row(index):
        own_columns = columns[index]

        def one_pair(count, running):
            left_slot = count // SLOTS
            right_slot = count % SLOTS
            middle = own_columns[left_slot]
            target = columns[middle, right_slot]
            meets = own_columns == target
            slot = jnp.argmax(meets).astype(jnp.int32)

            def added():
                product = jnp.dot(scaled_tile(index, left_slot).astype(jnp.float32), scaled_tile(middle, right_slot).astype(jnp.float32), preferred_element_type=jnp.float32)
                return lax.dynamic_update_index_in_dim(running, running[slot] + product, slot, 0)
            return lax.cond(jnp.any(meets), added, lambda: running)
        paths = lax.fori_loop(0, SLOTS * SLOTS, one_pair, jnp.zeros((SLOTS, TILE, TILE), jnp.float32))
        own_scaled = (tile_values[index].astype(jnp.float32) * scale[index][:, None, None]).astype(jnp.bfloat16)
        return (own_scaled.astype(jnp.float32) * paths).astype(jnp.bfloat16)
    motif = lax.map(motif_row, row_ids)
    degree = lax.optimization_barrier(jnp.sum(motif, axis=(1, 3), dtype=jnp.float32)).reshape(NODES)

    def apply_graph(vectors):
        pieces = vectors.reshape(NB, TILE, VEC)

        def one_row(index):

            def one_slot(slot, running):
                return running + jnp.dot(motif[index, slot].astype(jnp.float32), pieces[columns[index, slot]].astype(jnp.float32), preferred_element_type=jnp.float32)
            return lax.fori_loop(0, SLOTS, one_slot, jnp.zeros((TILE, VEC), jnp.float32))
        total = lax.map(one_row, row_ids).reshape(NODES, VEC)
        return total + degree[:, None] * vectors.astype(jnp.float32)
    basis = initial_vectors.astype(jnp.float32)
    for turn in range(2):
        current = (basis * lax.rsqrt(degree)[:, None]).astype(jnp.bfloat16)
        image = apply_graph(current)
        basis = orthonormal(image * lax.rsqrt(degree)[:, None])
    return basis
```

```python
import jax
import jax.numpy as jnp
from jax import lax
from jax.experimental import pallas as pl
from jax.experimental.pallas import tpu as pltpu
from jax.sharding import PartitionSpec as P

TILE = 256
VEC = 64
SLOTS = 6
REACH = 8
NODES = 131072
BLK = 32
CHIPS = 16
NX, NY, NZ = 4, 8, 8
HALF = 16
F32 = jnp.float32
BF16 = jnp.bfloat16
NEED = [min(SLOTS, REACH - d) for d in range(REACH)]
SHIP = {1: 6, 2: 5, 3: 3}
ROWS = {1: 6, 2: 6, 3: 5, 4: 5, 5: 3, 6: 3, 7: 1}
NT = (((1,), (1,)), ((), ()))


def power_of_two(e):
    one = jnp.float32(1.0)
    return jnp.where(
        e == -2, 0.25 * one,
        jnp.where(e == -1, 0.5 * one, jnp.where(e == 0, one, jnp.where(e == 1, 2 * one, 4 * one))),
    )


def dot32(a, b, dims=(((1,), (0,)), ((), ()))):
    return lax.dot_general(
        a, b, dims, precision=lax.Precision.HIGHEST, preferred_element_type=F32
    )


def eliminate(blocks, first, last):
    blocks = list(blocks)
    sub = lax.broadcasted_iota(jnp.int32, (8, 128), 0)
    for k in range(first, last):
        kb, kr = divmod(k, 8)
        pivot_row = blocks[kb][kr : kr + 1, :]
        inverse = 1.0 / pivot_row[:, k : k + 1]
        row = pivot_row * inverse
        for i in range(kb, 8):
            factor = blocks[i][:, k : k + 1]
            if i == kb:
                if kr == 7:
                    continue
                factor = jnp.where(sub[:, :1] > kr, factor, 0.0)
            blocks[i] = blocks[i] - factor * row
    return blocks


def finish(blocks):
    lane = lax.broadcasted_iota(jnp.int32, (8, 128), 1)
    sub = lax.broadcasted_iota(jnp.int32, (8, 128), 0)
    done = []
    for i, block in enumerate(blocks):
        pivot = jnp.sum(jnp.where(lane == sub + 8 * i, block, 0.0), axis=1, keepdims=True)
        done.append(block * lax.rsqrt(pivot))
    return jnp.concatenate(done, axis=0)


def kernel(
    tv, off, ex, v0, out,
    own, rb1, rb2, rb3, rb4, rb5, rb6, rb7, meta, smeta, paths, motif, xs1, xs2,
    g_src, ga, gb_src, gb, gc_src, gc, gd_src, gd, fin,
    own_sem, smeta_sem, ts, tr, ms, mr, x1s, x1r, x2s, x2r,
    gas, gar, gbs, gbr, gcs, gcr, gds, gdr, ges, ger,
):
    rb = {1: rb1, 2: rb2, 3: rb3, 4: rb4, 5: rb5, 6: rb6, 7: rb7}
    g = lax.axis_index("grp")
    b = lax.axis_index("blk")
    c = lax.rem(b, 2)
    q = b // 2
    x_hi, z = lax.rem(q, 2), q // 2
    x_lo, y = lax.rem(g, 2), g // 2
    x = x_hi * 2 + x_lo

    def at_blk(chip, core):
        return {"grp": g, "blk": lax.rem(chip + 2 * CHIPS, CHIPS) * 2 + core}

    def at_behind(d):
        return {"grp": g, "blk": lax.rem(b + BLK - d, BLK)}

    def at_xyz(xx, yy, zz):
        return {
            "grp": yy * 2 + lax.rem(xx, 2),
            "blk": (zz * 2 + xx // 2) * 2 + c,
        }

    sibling = at_blk(q, 1 - c)
    cross = at_blk(q - 4 + 8 * c, 1 - c)
    x_mates = [at_xyz(lax.rem(x + j, NX), y, z) for j in range(1, NX)]
    y_mates = [at_xyz(x, lax.rem(y + j, NY), z) for j in range(1, NY)]
    z_mates = [at_xyz(x, y, lax.rem(z + j, NZ)) for j in range(1, NZ)]

    def remote(src, dst, ssem, rsem, dev):
        return pltpu.make_async_remote_copy(
            src_ref=src, dst_ref=dst, send_sem=ssem, recv_sem=rsem,
            device_id=dev, device_id_type=pl.DeviceIdType.MESH,
        )

    load_own = pltpu.make_async_copy(tv.at[0], own, own_sem)
    load_own.start()

    offs = [off[0, s] for s in range(SLOTS)]
    exps = [ex[0, s] for s in range(SLOTS)]
    lane8 = lax.broadcasted_iota(jnp.int32, (8, 128), 1)
    note = jnp.zeros((8, 128), jnp.int32)
    for s in range(SLOTS):
        note = jnp.where(lane8 == s, offs[s], note)
        note = jnp.where(lane8 == 8 + s, exps[s], note)
    meta[0] = note

    barrier = pltpu.get_barrier_semaphore()
    met = x_mates + y_mates + z_mates
    for d in range(1, REACH):
        met.append(at_behind(d))
        met.append(at_behind(-d))
    for dev in met:
        pl.semaphore_signal(barrier, inc=1, device_id=dev, device_id_type=pl.DeviceIdType.MESH)
    pl.semaphore_wait(barrier, len(met))

    tile_out = [
        remote(tv.at[0, pl.ds(0, n)], rb[2 * k].at[pl.ds(0, n)], ts.at[k], tr.at[2 * k], at_blk(q - k, c))
        for k, n in SHIP.items()
    ]
    far_tile = remote(tv.at[0, pl.ds(0, 1)], rb[7], ts.at[4], tr.at[7], cross)
    near_tile = remote(tv.at[0], rb[1], ts.at[5], tr.at[1], sibling)
    note_out = [
        remote(meta.at[0], meta.at[d], ms.at[d], mr.at[d], at_behind(d)) for d in range(1, REACH)
    ]
    for copy in note_out:
        copy.start()
    for copy in tile_out:
        copy.start()

    @pl.when(c == 0)
    def _():
        far_tile.start()

    @pl.when(c == 1)
    def _():
        near_tile.start()

    load_own.wait()

    def hand_on(k):
        copies = []
        for core in range(2):
            d = 2 * k - 1 + 2 * core
            copies.append(
                remote(rb[2 * k].at[pl.ds(0, NEED[d])], rb[d], ts.at[5 + k], tr.at[d], sibling)
            )
        return copies

    def by_core(copies, act):
        for core in range(2):
            @pl.when(c == core)
            def _(copy=copies[core]):
                act(copy)

    def absorb(d, right_ref, first):
        slot = jnp.int32(0)
        grade = jnp.float32(0.0)
        for r in range(SLOTS):
            hit = offs[r] == d
            slot = jnp.where(hit, r, slot)
            grade = jnp.where(hit, power_of_two(exps[r]), grade)
        left = own[slot]

        def one(s, carry):
            wanted = smeta[0, 0, s] - d
            t = jnp.int32(0)
            scale = jnp.float32(0.0)
            for j in range(NEED[d]):
                hit = smeta[d, 0, j] == wanted
                t = jnp.where(hit, j, t)
                scale = jnp.where(hit, power_of_two(smeta[d, 0, 8 + j]), scale)
            product = jnp.dot(left, right_ref[t], preferred_element_type=F32) * (grade * scale)
            if first:
                paths[s] = product
            else:
                paths[s] = paths[s] + product
            return carry

        lax.fori_loop(0 if d == 0 else max(1, d - 2), SLOTS, one, 0)

    for copy in note_out:
        copy.wait_recv()
    to_scalar = pltpu.make_async_copy(meta, smeta, smeta_sem)
    to_scalar.start()
    to_scalar.wait()

    absorb(0, own, True)
    for k in range(1, 4):
        tile_out[k - 1].wait_recv()
        by_core(hand_on(k), lambda copy: copy.start())
        absorb(2 * k, rb[2 * k], False)
        d = 2 * k - 1
        remote(rb[d], rb[d], ts.at[0], tr.at[d], sibling).wait_recv()
        absorb(d, rb[d], False)
    remote(rb[7], rb[7], ts.at[0], tr.at[7], sibling).wait_recv()
    absorb(7, rb[7], False)

    ones = jnp.ones((8, TILE), BF16)
    degree = jnp.zeros((8, TILE), F32)
    for s in range(SLOTS):
        tile = ((own[s].astype(F32) * power_of_two(exps[s])) * paths[s]).astype(BF16)
        motif[s] = tile
        degree = degree + lax.dot_general(ones, tile, NT, preferred_element_type=F32)
    degree = degree[0:1, :]
    root = lax.rsqrt(degree)

    def exchange(xs, ssem, rsem):
        direct = [remote(xs.at[0], xs.at[2 * k], ssem.at[k], rsem.at[2 * k], at_blk(q - k, c)) for k in (1, 2, 3)]
        far = remote(xs.at[0], xs.at[7], ssem.at[4], rsem.at[7], cross)
        near = remote(xs.at[0], xs.at[1], ssem.at[5], rsem.at[1], sibling)

        @pl.when(c == 0)
        def _():
            far.start()

        @pl.when(c == 1)
        def _():
            near.start()

        for copy in direct:
            copy.start()
        return direct, far, near

    def passing(xs, ssem, rsem, k):
        return [
            remote(xs.at[2 * k], xs.at[2 * k - 1 + 2 * core], ssem.at[5 + k], rsem.at[2 * k - 1 + 2 * core], sibling)
            for core in range(2)
        ]

    def relay(xs, ssem, rsem, direct):
        for k in (1, 2, 3):
            direct[k - 1].wait_recv()
            by_core(passing(xs, ssem, rsem, k), lambda copy: copy.start())
        for d in (1, 3, 5, 7):
            remote(xs.at[d], xs.at[d], ssem.at[0], rsem.at[d], sibling).wait_recv()

    def apply_graph(xs):
        total = jnp.zeros((VEC, TILE), F32)
        for s in range(SLOTS):
            total = total + lax.dot_general(xs[offs[s]], motif[s], NT, preferred_element_type=F32)
        return total

    lane = lax.broadcasted_iota(jnp.int32, (64, 128), 1)
    row = lax.broadcasted_iota(jnp.int32, (64, 128), 0)
    left = lane < VEC
    zeros = jnp.zeros((64, 128), F32)

    def gram(i, vectors):
        both = dot32(vectors, jnp.concatenate([vectors, vectors], axis=0), NT)
        g_src[i] = jnp.where(left[:32], both[:32], both[32:]) / NODES

    def copies_a(i):
        return [remote(g_src.at[i, pl.ds((1 - c) * HALF, HALF)], ga.at[i], gas.at[i], gar.at[i], sibling)]

    def copies_b(i):
        return [remote(gb_src.at[i], gb.at[i, j], gbs.at[i, j], gbr.at[i, j], x_mates[j]) for j in range(NX - 1)]

    def copies_c(i):
        return [remote(gc_src.at[i], gc.at[i, j], gcs.at[i, j], gcr.at[i, j], y_mates[j]) for j in range(NY - 1)]

    def copies_d(i):
        return [remote(gd_src.at[i], gd.at[i, j], gds.at[i, j], gdr.at[i, j], z_mates[j]) for j in range(NZ - 1)]

    def copies_e(i):
        mine = pl.ds(c * HALF, HALF)
        return [remote(fin.at[i, mine], fin.at[i, mine], ges.at[i], ger.at[i], sibling)]

    def start(copies):
        for copy in copies:
            copy.start()

    def arrive(copies):
        for copy in copies:
            copy.wait_recv()

    def step_a(i):
        start(copies_a(i))

    def step_b(i):
        arrive(copies_a(i))
        gb_src[i] = g_src[i, pl.ds(c * HALF, HALF), :] + ga[i]
        start(copies_b(i))

    def step_c(i):
        arrive(copies_b(i))
        gc_src[i] = gb_src[i] + (gb[i, 0] + gb[i, 1] + gb[i, 2])
        start(copies_c(i))

    def step_d(i):
        arrive(copies_c(i))
        gd_src[i] = gc_src[i] + sum(gc[i, j] for j in range(1, 7)) + gc[i, 0]
        start(copies_d(i))

    def step_e(i):
        arrive(copies_d(i))
        fin[i, pl.ds(c * HALF, HALF), :] = gd_src[i] + sum(gd[i, j] for j in range(1, 7)) + gd[i, 0]
        start(copies_e(i))

    def collect(i):
        other = pl.ds((1 - c) * HALF, HALF)
        remote(fin.at[i, other], fin.at[i, other], ges.at[i], ger.at[i], sibling).wait_recv()
        packed = fin[i]
        turned = pltpu.roll(packed, 64, 1)
        return jnp.concatenate(
            [jnp.where(left[:32], packed, turned), jnp.where(left[:32], turned, packed)], axis=0
        )

    unit = (
        lax.broadcasted_iota(jnp.int32, (VEC, VEC), 0) == lax.broadcasted_iota(jnp.int32, (VEC, VEC), 1)
    ).astype(BF16)
    start_t = lax.dot_general(unit, v0[...], NT, preferred_element_type=F32)
    input_1 = (start_t * root).astype(BF16)
    xs1[0] = input_1
    sent_1 = exchange(xs1, x1s, x1r)
    relay(xs1, x1s, x1r, sent_1[0])
    scaled_1 = (apply_graph(xs1) + degree * input_1.astype(F32)) * root

    wide_2 = scaled_1 * root
    xs2[0] = wide_2.astype(BF16)
    sent_2 = exchange(xs2, x2s, x2r)
    gram(0, scaled_1)
    step_a(0)
    step_b(0)
    relay(xs2, x2s, x2r, sent_2[0])
    step_c(0)
    scaled_2 = (apply_graph(xs2) + degree * wide_2) * root
    gram(1, scaled_2)
    step_a(1)
    step_d(0)
    step_b(1)
    step_e(0)
    gram_1 = collect(0)
    step_c(1)
    augmented = jnp.where(left, gram_1, jnp.where(lane == row + VEC, 1.0, 0.0))
    blocks = [augmented[8 * i : 8 * i + 8] for i in range(8)]
    blocks = eliminate(blocks, 0, 24)
    step_d(1)
    blocks = eliminate(blocks, 24, VEC)
    inverse_1 = jnp.where(left, 0.0, finish(blocks))
    step_e(1)
    gram_2 = jnp.where(left, 0.0, collect(1))
    half_way = dot32(inverse_1, jnp.concatenate([zeros, gram_2], axis=0))
    middle = dot32(half_way, jnp.concatenate([inverse_1, zeros], axis=0), NT)
    augmented = jnp.where(left, middle, inverse_1)
    blocks = eliminate([augmented[8 * i : 8 * i + 8] for i in range(8)], 0, VEC)
    inverse_2 = jnp.where(left, 0.0, finish(blocks))
    out[...] = dot32(inverse_2, jnp.concatenate([jnp.zeros((VEC, TILE), F32), scaled_2], axis=0))

    for copy in note_out + tile_out + sent_1[0] + sent_2[0]:
        copy.wait_send()

    @pl.when(c == 0)
    def _():
        far_tile.wait_send()
        sent_1[1].wait_send()
        sent_2[1].wait_send()

    @pl.when(c == 1)
    def _():
        near_tile.wait_send()
        sent_1[2].wait_send()
        sent_2[2].wait_send()

    for k in (1, 2, 3):
        by_core(hand_on(k), lambda copy: copy.wait_send())
        by_core(passing(xs1, x1s, x1r, k), lambda copy: copy.wait_send())
        by_core(passing(xs2, x2s, x2r, k), lambda copy: copy.wait_send())
    for i in range(2):
        for copies in (copies_a, copies_b, copies_c, copies_d, copies_e):
            for copy in copies(i):
                copy.wait_send()


def shards(tile_values, tile_offset, tile_exponent, initial_vectors):
    dma = pltpu.SemaphoreType.DMA
    tiles = [pltpu.VMEM((ROWS[d], TILE, TILE), BF16) for d in range(1, REACH)]
    basis_t = pl.pallas_call(
        kernel,
        out_shape=jax.ShapeDtypeStruct((VEC, TILE), F32),
        in_specs=[
            pl.BlockSpec(memory_space=pl.ANY),
            pl.BlockSpec(memory_space=pltpu.SMEM),
            pl.BlockSpec(memory_space=pltpu.SMEM),
            pl.BlockSpec(memory_space=pltpu.VMEM),
        ],
        out_specs=pl.BlockSpec(memory_space=pltpu.VMEM),
        scratch_shapes=[
            pltpu.VMEM((SLOTS, TILE, TILE), BF16),
            *tiles,
            pltpu.VMEM((REACH, 8, 128), jnp.int32),
            pltpu.SMEM((REACH, 8, 128), jnp.int32),
            pltpu.VMEM((SLOTS, TILE, TILE), F32),
            pltpu.VMEM((SLOTS, TILE, TILE), BF16),
            pltpu.VMEM((REACH, VEC, TILE), BF16),
            pltpu.VMEM((REACH, VEC, TILE), BF16),
            pltpu.VMEM((2, 2 * HALF, 128), F32),
            pltpu.VMEM((2, HALF, 128), F32),
            pltpu.VMEM((2, HALF, 128), F32),
            pltpu.VMEM((2, NX - 1, HALF, 128), F32),
            pltpu.VMEM((2, HALF, 128), F32),
            pltpu.VMEM((2, NY - 1, HALF, 128), F32),
            pltpu.VMEM((2, HALF, 128), F32),
            pltpu.VMEM((2, NZ - 1, HALF, 128), F32),
            pltpu.VMEM((2, 2 * HALF, 128), F32),
            dma, dma,
            dma((9,)), dma((8,)),
            dma((8,)), dma((8,)),
            dma((9,)), dma((8,)),
            dma((9,)), dma((8,)),
            dma((2,)), dma((2,)),
            dma((2, NX - 1)), dma((2, NX - 1)),
            dma((2, NY - 1)), dma((2, NY - 1)),
            dma((2, NZ - 1)), dma((2, NZ - 1)),
            dma((2,)), dma((2,)),
        ],
        compiler_params=pltpu.CompilerParams(
            collective_id=0, has_side_effects=True, vmem_limit_bytes=40 * 1024 * 1024
        ),
        cost_estimate=pl.CostEstimate(flops=1200000000, bytes_accessed=1000000, transcendentals=0),
        name="embed",
    )(tile_values, tile_offset, tile_exponent, initial_vectors)
    return basis_t.T


def solution(mesh):
    return jax.shard_map(
        shards,
        mesh=mesh,
        in_specs=(
            P(("grp", "blk"), None, None, None),
            P(("grp", "blk"), None),
            P(("grp", "blk"), None),
            P(("grp", "blk"), None),
        ),
        out_specs=P(("grp", "blk"), None),
        check_vma=False,
    )
```

```python
import jax
import jax.numpy as jnp
from jax import lax
from jax.experimental import pallas as pl
from jax.experimental.pallas import tpu as pltpu
from jax.sharding import PartitionSpec as P

TILE = 256
VEC = 64
SLOTS = 6
REACH = 8
NODES = 131072
BLK = 32
CHIPS = 16
NX, NY, NZ = 4, 8, 8
HALF = 16
F32 = jnp.float32
BF16 = jnp.bfloat16
NEED = [min(SLOTS, REACH - d) for d in range(REACH)]
PIECES = [(0, 1), (1, 3), (3, 5), (5, 6)]
PARTS = {1: [(0, 3), (3, 6)], 3: [(0, 3), (3, 5)], 5: [(0, 3)], 7: [(0, 1)]}
ROWS = {1: 6, 2: 6, 3: 5, 4: 6, 5: 3, 6: 3, 7: 1}
NT = (((1,), (1,)), ((), ()))


def power_of_two(e):
    one = jnp.float32(1.0)
    return jnp.where(
        e == -2, 0.25 * one,
        jnp.where(e == -1, 0.5 * one, jnp.where(e == 0, one, jnp.where(e == 1, 2 * one, 4 * one))),
    )


def dot32(a, b, dims=(((1,), (0,)), ((), ()))):
    return lax.dot_general(
        a, b, dims, precision=lax.Precision.HIGHEST, preferred_element_type=F32
    )


def eliminate(blocks, first, last):
    blocks = list(blocks)
    sub = lax.broadcasted_iota(jnp.int32, (8, 128), 0)

    def spread(row):
        return jnp.broadcast_to(row, (8, 128))

    for k in range(first, last, 4):
        kb, kr = divmod(k, 8)
        head = blocks[kb]
        columns = {
            i: [spread(blocks[i][:, k + j : k + j + 1]) for j in range(4)]
            for i in range(kb, 8)
        }
        upper = [spread(head[kr + j : kr + j + 1, :]) for j in range(4)]
        corner = [[spread(columns[kb][j][kr + a : kr + a + 1, :]) for j in range(4)] for a in range(4)]
        inverse = []
        for a in range(4):
            inverse.append(1.0 / corner[a][a])
            for r in range(a + 1, 4):
                low = corner[a][r] * inverse[a]
                for j in range(r, 4):
                    corner[r][j] = corner[r][j] - low * corner[a][j]
                upper[r] = upper[r] - low * upper[a]
        for i in range(kb, 8):
            if i == kb and kr == 4:
                continue
            block = blocks[i]
            factors = []
            for a in range(4):
                rest = columns[i][a]
                for e in range(a):
                    rest = rest - factors[e] * corner[e][a]
                factors.append(rest * inverse[a])
            for a in range(4):
                block = block - factors[a] * upper[a]
            blocks[i] = block if i > kb else jnp.where(sub > kr + 3, block, head)
        done = blocks[kb]
        for a in range(4):
            done = jnp.where(sub == kr + a, upper[a], done)
        blocks[kb] = done
    return blocks


def finish(blocks):
    lane = lax.broadcasted_iota(jnp.int32, (8, 128), 1)
    sub = lax.broadcasted_iota(jnp.int32, (8, 128), 0)
    done = []
    for i, block in enumerate(blocks):
        pivot = jnp.sum(jnp.where(lane == sub + 8 * i, block, 0.0), axis=1, keepdims=True)
        done.append(block * lax.rsqrt(pivot))
    return jnp.concatenate(done, axis=0)


def kernel(
    tv, off_any, ex_any, v0, out,
    own, rb1, rb2, rb3, rb4, rb5, rb6, rb7, off, ex, meta, smeta, paths, motif, xs1, xs2,
    g_src, gb, gc_src, gc, gd_src, gd, fin,
    own_sem, in_sem, smeta_sem, ts, tr, ms, mr, x1s, x1r, x2s, x2r,
    gbs, gbr, gcs, gcr, gds, gdr, ges, ger,
):
    rb = {1: rb1, 2: rb2, 3: rb3, 4: rb4, 5: rb5, 6: rb6, 7: rb7}
    g = lax.axis_index("grp")
    b = lax.axis_index("blk")
    c = lax.rem(b, 2)
    q = b // 2
    x_hi, z = lax.rem(q, 2), q // 2
    x_lo, y = lax.rem(g, 2), g // 2
    x = x_hi * 2 + x_lo

    def at_blk(chip, core):
        return {"grp": g, "blk": lax.rem(chip + 2 * CHIPS, CHIPS) * 2 + core}

    def at_behind(d):
        return {"grp": g, "blk": lax.rem(b + BLK - d, BLK)}

    def at_xyz(xx, yy, zz, core=c):
        return {
            "grp": yy * 2 + lax.rem(xx, 2),
            "blk": (zz * 2 + xx // 2) * 2 + core,
        }

    sibling = at_blk(q, 1 - c)
    cross = at_blk(q - 4 + 8 * c, 1 - c)
    facing = at_blk(q + 1 - 2 * x_hi, c)
    below = at_blk(q - 2, c)
    x_mates = [at_xyz(lax.rem(x + j, NX), y, z) for j in range(1, NX)]
    x_others = [at_xyz(lax.rem(x + j, NX), y, z, 1 - c) for j in range(NX)]
    y_mates = [at_xyz(x, lax.rem(y + j, NY), z) for j in range(1, NY)]
    z_mates = [at_xyz(x, y, lax.rem(z + j, NZ)) for j in range(1, NZ)]

    def remote(src, dst, ssem, rsem, dev):
        return pltpu.make_async_remote_copy(
            src_ref=src, dst_ref=dst, send_sem=ssem, recv_sem=rsem,
            device_id=dev, device_id_type=pl.DeviceIdType.MESH,
        )

    load_own = pltpu.make_async_copy(tv.at[0], own, own_sem)
    load_own.start()
    load_off = pltpu.make_async_copy(off_any, off, in_sem.at[0])
    load_ex = pltpu.make_async_copy(ex_any, ex, in_sem.at[1])
    load_off.start()
    load_ex.start()

    barrier = pltpu.get_barrier_semaphore()
    met = x_mates + x_others[1:] + y_mates + z_mates
    for d in range(1, REACH):
        met.append(at_behind(d))
        met.append(at_behind(-d))
    for dev in met:
        pl.semaphore_signal(barrier, inc=1, device_id=dev, device_id_type=pl.DeviceIdType.MESH)
    load_off.wait()
    load_ex.wait()
    offs = [off[0, s] for s in range(SLOTS)]
    exps = [ex[0, s] for s in range(SLOTS)]
    lane8 = lax.broadcasted_iota(jnp.int32, (8, 128), 1)
    note = jnp.zeros((8, 128), jnp.int32)
    for s in range(SLOTS):
        note = jnp.where(lane8 == s, offs[s], note)
        note = jnp.where(lane8 == 8 + s, exps[s], note)
    meta[0] = note
    pl.semaphore_wait(barrier, len(met))

    def piece(src, d, j, sem, dev):
        lo, hi = PIECES[j]
        return remote(src.at[pl.ds(lo, hi - lo)], rb[d].at[pl.ds(lo, hi - lo)], ts.at[sem + j], tr.at[d, j], dev)

    mine = tv.at[0]
    own_down = [piece(mine, 4, j, 0, below) for j in range(4)]
    own_facing = [piece(mine, 2, j, 4, facing) for j in range(4)]
    on_facing = [piece(rb4, 2, j, 4, facing) for j in range(4)]
    on_down = [piece(rb2, 6, j, 8, below) for j in range(2)]
    far_tile = remote(tv.at[0, pl.ds(0, 1)], rb7, ts.at[10], tr.at[7, 0], cross)

    def part(src, d, p, sem):
        lo, hi = PARTS[d][p]
        return remote(src.at[pl.ds(lo, hi - lo)], rb[d].at[pl.ds(lo, hi - lo)], ts.at[sem + p], tr.at[d, p], sibling)

    near_tiles = [part(mine, 1, p, 11) for p in range(2)]
    note_out = [
        remote(meta.at[0], meta.at[d], ms.at[d], mr.at[d], at_behind(d)) for d in range(1, REACH)
    ]
    even, odd = x_hi == 0, x_hi == 1
    for copy in note_out:
        copy.start()

    @pl.when(even)
    def _():
        for j in range(4):
            own_down[j].start()

    @pl.when(odd)
    def _():
        for j in range(4):
            own_facing[j].start()
            if j < 3:
                own_down[j].start()

    @pl.when(c == 1)
    def _():
        for copy in near_tiles:
            copy.start()

    @pl.when(c == 0)
    def _():
        far_tile.start()

    def hand_on(k, p):
        return [
            part(rb[2 * k], d, p, 11 + 2 * k) if p < len(PARTS[d]) else None
            for d in (2 * k - 1, 2 * k + 1)
        ]

    def by_core(copies, act):
        for core in range(2):
            if copies[core] is not None:
                @pl.when(c == core)
                def _(copy=copies[core]):
                    act(copy)

    def go(copy):
        copy.start()

    def left_here(copy):
        copy.wait_send()

    def here(d):
        for p in range(len(PARTS[d])):
            part(rb[d], d, p, 11).wait_recv()

    def absorb(d, right_ref, first):
        slot = jnp.int32(0)
        grade = jnp.float32(0.0)
        for r in range(SLOTS):
            hit = offs[r] == d
            slot = jnp.where(hit, r, slot)
            grade = jnp.where(hit, power_of_two(exps[r]), grade)
        left = own[slot]

        def one(s, carry):
            wanted = smeta[0, 0, s] - d
            t = jnp.int32(0)
            scale = jnp.float32(0.0)
            for j in range(NEED[d]):
                hit = smeta[d, 0, j] == wanted
                t = jnp.where(hit, j, t)
                scale = jnp.where(hit, power_of_two(smeta[d, 0, 8 + j]), scale)
            product = jnp.dot(left, right_ref[t], preferred_element_type=F32) * (grade * scale)
            if first:
                paths[s] = product
            else:
                paths[s] = paths[s] + product
            return carry

        lax.fori_loop(0 if d == 0 else max(1, d - 2), SLOTS, one, 0)

    for j in range(4):
        if j < 3:
            own_down[j].wait_recv()

        @pl.when(even)
        def _(j=j):
            if j == 3:
                own_down[j].wait_recv()
            on_facing[j].start()

        own_facing[j].wait_recv()
        if j < 2:
            on_down[j].start()
        if j == 1:
            by_core(hand_on(1, 0), go)
            by_core(hand_on(2, 0), go)
            for copy in note_out:
                copy.wait_recv()
            to_scalar = pltpu.make_async_copy(meta, smeta, smeta_sem)
            to_scalar.start()
            to_scalar.wait()
            load_own.wait()
            absorb(0, own, True)
        if j == 2:
            by_core(hand_on(2, 1), go)
    by_core(hand_on(1, 1), go)
    absorb(4, rb4, False)
    absorb(2, rb2, False)
    for j in range(2):
        on_down[j].wait_recv()
    by_core(hand_on(3, 0), go)
    absorb(6, rb6, False)
    for d in (1, 3, 5, 7):
        here(d)
        absorb(d, rb[d], False)

    ones = jnp.ones((8, TILE), BF16)
    degree = jnp.zeros((8, TILE), F32)
    for s in range(SLOTS):
        tile = ((own[s].astype(F32) * power_of_two(exps[s])) * paths[s]).astype(BF16)
        motif[s] = tile
        degree = degree + lax.dot_general(ones, tile, NT, preferred_element_type=F32)
    degree = degree[0:1, :]
    root = lax.rsqrt(degree)

    def exchange(xs, ssem, rsem):
        return [remote(xs.at[0], xs.at[d], ssem.at[d], rsem.at[d], at_behind(d)) for d in range(1, REACH)]

    def apply_graph(xs):
        total = jnp.zeros((VEC, TILE), F32)
        for s in range(SLOTS):
            total = total + lax.dot_general(xs[offs[s]], motif[s], NT, preferred_element_type=F32)
        return total

    lane = lax.broadcasted_iota(jnp.int32, (64, 128), 1)
    row = lax.broadcasted_iota(jnp.int32, (64, 128), 0)
    left = lane < VEC
    zeros = jnp.zeros((64, 128), F32)

    def gram(i, vectors):
        both = dot32(vectors, jnp.concatenate([vectors, vectors], axis=0), NT)
        g_src[i] = jnp.where(left[:32], both[:32], both[32:]) / NODES

    def copies_b(i):
        own_half, other_half = pl.ds(c * HALF, HALF), pl.ds((1 - c) * HALF, HALF)
        return [
            remote(g_src.at[i, other_half], gb.at[i, 3 + j], gbs.at[i, 3 + j], gbr.at[i, 3 + j], x_others[j])
            for j in range(NX)
        ] + [
            remote(g_src.at[i, own_half], gb.at[i, j], gbs.at[i, j], gbr.at[i, j], x_mates[j])
            for j in range(NX - 1)
        ]

    def copies_c(i):
        return [remote(gc_src.at[i], gc.at[i, j], gcs.at[i, j], gcr.at[i, j], y_mates[j]) for j in range(NY - 1)]

    def copies_d(i):
        return [remote(gd_src.at[i], gd.at[i, j], gds.at[i, j], gdr.at[i, j], z_mates[j]) for j in range(NZ - 1)]

    def copies_e(i):
        mine = pl.ds(c * HALF, HALF)
        return [remote(fin.at[i, mine], fin.at[i, mine], ges.at[i], ger.at[i], sibling)]

    def start(copies):
        for copy in copies:
            copy.start()

    def arrive(copies):
        for copy in copies:
            copy.wait_recv()

    def step_b(i):
        start(copies_b(i))

    def step_c(i):
        arrive(copies_b(i))
        gc_src[i] = g_src[i, pl.ds(c * HALF, HALF), :] + sum(gb[i, j] for j in range(1, 7)) + gb[i, 0]
        start(copies_c(i))

    def step_d(i):
        arrive(copies_c(i))
        gd_src[i] = gc_src[i] + sum(gc[i, j] for j in range(1, 7)) + gc[i, 0]
        start(copies_d(i))

    def step_e(i):
        arrive(copies_d(i))
        fin[i, pl.ds(c * HALF, HALF), :] = gd_src[i] + sum(gd[i, j] for j in range(1, 7)) + gd[i, 0]
        start(copies_e(i))

    def collect(i):
        other = pl.ds((1 - c) * HALF, HALF)
        remote(fin.at[i, other], fin.at[i, other], ges.at[i], ger.at[i], sibling).wait_recv()
        packed = fin[i]
        turned = pltpu.roll(packed, 64, 1)
        return jnp.concatenate(
            [jnp.where(left[:32], packed, turned), jnp.where(left[:32], turned, packed)], axis=0
        )

    input_1 = (v0[...].astype(F32) * root).astype(BF16)
    xs1[0] = input_1
    sent_1 = exchange(xs1, x1s, x1r)
    start(sent_1)
    arrive(sent_1)
    scaled_1 = (apply_graph(xs1) + degree * input_1.astype(F32)) * root

    wide_2 = scaled_1 * root
    xs2[0] = wide_2.astype(BF16)
    sent_2 = exchange(xs2, x2s, x2r)
    start(sent_2)
    gram(0, scaled_1)
    step_b(0)
    step_c(0)
    step_d(0)
    arrive(sent_2)
    scaled_2 = (apply_graph(xs2) + degree * wide_2) * root
    gram(1, scaled_2)
    step_b(1)
    step_e(0)
    step_c(1)
    gram_1 = collect(0)
    augmented = jnp.where(left, gram_1, jnp.where(lane == row + VEC, 1.0, 0.0))
    blocks = [augmented[8 * i : 8 * i + 8] for i in range(8)]
    blocks = eliminate(blocks, 0, 32)
    step_d(1)
    blocks = eliminate(blocks, 32, VEC)
    inverse_1 = jnp.where(left, 0.0, finish(blocks))
    step_e(1)
    gram_2 = jnp.where(left, 0.0, collect(1))
    half_way = dot32(inverse_1, jnp.concatenate([zeros, gram_2], axis=0))
    middle = dot32(half_way, jnp.concatenate([inverse_1, zeros], axis=0), NT)
    augmented = jnp.where(left, middle, inverse_1)
    blocks = eliminate([augmented[8 * i : 8 * i + 8] for i in range(8)], 0, VEC)
    inverse_2 = jnp.where(left, 0.0, finish(blocks))
    out[...] = dot32(inverse_2, jnp.concatenate([jnp.zeros((VEC, TILE), F32), scaled_2], axis=0))

    for copy in note_out + sent_1 + sent_2 + own_down[:3] + own_facing + on_down:
        copy.wait_send()

    @pl.when(even)
    def _():
        own_down[3].wait_send()

    @pl.when(c == 0)
    def _():
        far_tile.wait_send()

    @pl.when(c == 1)
    def _():
        for copy in near_tiles:
            copy.wait_send()

    for k in (1, 2, 3):
        for p in range(2):
            by_core(hand_on(k, p), left_here)
    for i in range(2):
        for copies in (copies_b, copies_c, copies_d, copies_e):
            for copy in copies(i):
                copy.wait_send()


def shards(tile_values, tile_offset, tile_exponent, initial_vectors):
    dma = pltpu.SemaphoreType.DMA
    tiles = [pltpu.VMEM((ROWS[d], TILE, TILE), BF16) for d in range(1, REACH)]
    basis_t = pl.pallas_call(
        kernel,
        out_shape=jax.ShapeDtypeStruct((VEC, TILE), F32),
        in_specs=[
            pl.BlockSpec(memory_space=pltpu.HBM),
            pl.BlockSpec(memory_space=pltpu.HBM),
            pl.BlockSpec(memory_space=pltpu.HBM),
            pl.BlockSpec(memory_space=pltpu.VMEM),
        ],
        out_specs=pl.BlockSpec(memory_space=pltpu.VMEM),
        scratch_shapes=[
            pltpu.VMEM((SLOTS, TILE, TILE), BF16),
            *tiles,
            pltpu.SMEM((1, SLOTS), jnp.int32),
            pltpu.SMEM((1, SLOTS), jnp.int32),
            pltpu.VMEM((REACH, 8, 128), jnp.int32),
            pltpu.SMEM((REACH, 8, 128), jnp.int32),
            pltpu.VMEM((SLOTS, TILE, TILE), F32),
            pltpu.VMEM((SLOTS, TILE, TILE), BF16),
            pltpu.VMEM((REACH, VEC, TILE), BF16),
            pltpu.VMEM((REACH, VEC, TILE), BF16),
            pltpu.VMEM((2, 2 * HALF, 128), F32),
            pltpu.VMEM((2, 2 * NX - 1, HALF, 128), F32),
            pltpu.VMEM((2, HALF, 128), F32),
            pltpu.VMEM((2, NY - 1, HALF, 128), F32),
            pltpu.VMEM((2, HALF, 128), F32),
            pltpu.VMEM((2, NZ - 1, HALF, 128), F32),
            pltpu.VMEM((2, 2 * HALF, 128), F32),
            dma, dma((2,)), dma,
            dma((20,)), dma((8, 4)),
            dma((8,)), dma((8,)),
            dma((8,)), dma((8,)),
            dma((8,)), dma((8,)),
            dma((2, 2 * NX - 1)), dma((2, 2 * NX - 1)),
            dma((2, NY - 1)), dma((2, NY - 1)),
            dma((2, NZ - 1)), dma((2, NZ - 1)),
            dma((2,)), dma((2,)),
        ],
        compiler_params=pltpu.CompilerParams(
            collective_id=0, has_side_effects=True, vmem_limit_bytes=40 * 1024 * 1024
        ),
        cost_estimate=pl.CostEstimate(flops=1200000000, bytes_accessed=1000000, transcendentals=0),
        name="embed",
    )(tile_values, tile_offset, tile_exponent, initial_vectors.T)
    return basis_t.T


def solution(mesh):
    return jax.shard_map(
        shards,
        mesh=mesh,
        in_specs=(
            P(("grp", "blk"), None, None, None),
            P(("grp", "blk"), None),
            P(("grp", "blk"), None),
            P(("grp", "blk"), None),
        ),
        out_specs=P(("grp", "blk"), None),
        check_vma=False,
    )
```

```python
import jax
import jax.numpy as jnp
from jax import lax
from jax.experimental import pallas as pl
from jax.experimental.pallas import tpu as pltpu
from jax.sharding import PartitionSpec as P

TILE = 256
VEC = 64
SLOTS = 6
REACH = 8
NODES = 131072
BLK = 32
CHIPS = 16
NX, NY, NZ = 4, 8, 8
HALF = 16
F32 = jnp.float32
BF16 = jnp.bfloat16
NEED = [min(SLOTS, REACH - d) for d in range(REACH)]
SECOND = [5, 4]
THIRD = [3, 2]
ACROSS = (1, 2)
PARTS = {1: [(0, 3), (3, 6)], 3: [(0, 3), (3, 5)], 5: [(0, 3)], 7: [(0, 1)]}
ROWS = {1: 6, 2: 6, 3: 5, 4: 6, 5: 3, 6: 3, 7: 1}
NT = (((1,), (1,)), ((), ()))


def power_of_two(e):
    one = jnp.float32(1.0)
    return jnp.where(
        e == -2, 0.25 * one,
        jnp.where(e == -1, 0.5 * one, jnp.where(e == 0, one, jnp.where(e == 1, 2 * one, 4 * one))),
    )


def dot32(a, b, dims=(((1,), (0,)), ((), ()))):
    return lax.dot_general(
        a, b, dims, precision=lax.Precision.HIGHEST, preferred_element_type=F32
    )


def eliminate(blocks, first, last):
    blocks = list(blocks)
    sub = lax.broadcasted_iota(jnp.int32, (8, 128), 0)

    def spread(row):
        return jnp.broadcast_to(row, (8, 128))

    for k in range(first, last, 4):
        kb, kr = divmod(k, 8)
        head = blocks[kb]
        columns = {
            i: [spread(blocks[i][:, k + j : k + j + 1]) for j in range(4)]
            for i in range(kb, 8)
        }
        upper = [spread(head[kr + j : kr + j + 1, :]) for j in range(4)]
        corner = [[spread(columns[kb][j][kr + a : kr + a + 1, :]) for j in range(4)] for a in range(4)]
        inverse = []
        for a in range(4):
            inverse.append(1.0 / corner[a][a])
            for r in range(a + 1, 4):
                low = corner[a][r] * inverse[a]
                for j in range(r, 4):
                    corner[r][j] = corner[r][j] - low * corner[a][j]
                upper[r] = upper[r] - low * upper[a]
        for i in range(kb, 8):
            if i == kb and kr == 4:
                continue
            block = blocks[i]
            factors = []
            for a in range(4):
                rest = columns[i][a]
                for e in range(a):
                    rest = rest - factors[e] * corner[e][a]
                factors.append(rest * inverse[a])
            for a in range(4):
                block = block - factors[a] * upper[a]
            blocks[i] = block if i > kb else jnp.where(sub > kr + 3, block, head)
        done = blocks[kb]
        for a in range(4):
            done = jnp.where(sub == kr + a, upper[a], done)
        blocks[kb] = done
    return blocks


def finish(blocks):
    lane = lax.broadcasted_iota(jnp.int32, (8, 128), 1)
    sub = lax.broadcasted_iota(jnp.int32, (8, 128), 0)
    done = []
    for i, block in enumerate(blocks):
        pivot = jnp.sum(jnp.where(lane == sub + 8 * i, block, 0.0), axis=1, keepdims=True)
        done.append(block * lax.rsqrt(pivot))
    return jnp.concatenate(done, axis=0)


def kernel(
    tv, off_any, ex_any, v0, out,
    own, rb1, rb2, rb3, rb4, rb5, rb6, rb7, off, ex, meta, smeta, paths, motif, vs, roots, xs2,
    g_src, gb, gc_src, gc, gd_src, gd, fin,
    own_sem, in_sem, smeta_sem, ts, tr, tp, ms, mr, vsend, vrecv, rsend, rrecv, x2s, x2r,
    gbs, gbr, gcs, gcr, gds, gdr, ges, ger,
):
    rb = {1: rb1, 2: rb2, 3: rb3, 4: rb4, 5: rb5, 6: rb6, 7: rb7}
    g = lax.axis_index("grp")
    b = lax.axis_index("blk")
    c = lax.rem(b, 2)
    q = b // 2
    x_hi, z = lax.rem(q, 2), q // 2
    x_lo, y = lax.rem(g, 2), g // 2
    x = x_hi * 2 + x_lo

    def at_blk(chip, core):
        return {"grp": g, "blk": lax.rem(chip + 2 * CHIPS, CHIPS) * 2 + core}

    def at_behind(d):
        return {"grp": g, "blk": lax.rem(b + BLK - d, BLK)}

    def at_xyz(xx, yy, zz, core=c):
        return {
            "grp": yy * 2 + lax.rem(xx, 2),
            "blk": (zz * 2 + xx // 2) * 2 + core,
        }

    sibling = at_blk(q, 1 - c)
    cross = at_blk(q - 4 + 8 * c, 1 - c)
    facing = at_blk(q + 1 - 2 * x_hi, c)
    even, odd = x_hi == 0, x_hi == 1
    below = at_blk(q - 2, c)
    x_mates = [at_xyz(lax.rem(x + j, NX), y, z) for j in range(1, NX)]
    x_others = [at_xyz(lax.rem(x + j, NX), y, z, 1 - c) for j in range(NX)]
    y_mates = [at_xyz(x, lax.rem(y + j, NY), z) for j in range(1, NY)]
    z_mates = [at_xyz(x, y, lax.rem(z + j, NZ)) for j in range(1, NZ)]

    def remote(src, dst, ssem, rsem, dev):
        return pltpu.make_async_remote_copy(
            src_ref=src, dst_ref=dst, send_sem=ssem, recv_sem=rsem,
            device_id=dev, device_id_type=pl.DeviceIdType.MESH,
        )

    load_own = pltpu.make_async_copy(tv.at[0], own, own_sem)
    load_own.start()
    load_off = pltpu.make_async_copy(off_any, off, in_sem.at[0])
    load_ex = pltpu.make_async_copy(ex_any, ex, in_sem.at[1])
    load_off.start()
    load_ex.start()
    load_v0 = pltpu.make_async_copy(v0, vs.at[0], in_sem.at[2])
    load_v0.start()

    barrier = pltpu.get_barrier_semaphore()
    met = [x_mates[0], x_mates[2], x_others[1], x_others[3]] + y_mates + z_mates[1:-1]
    for d in range(1, REACH):
        met.append(at_behind(d))
        met.append(at_behind(-d))
    for dev in met:
        pl.semaphore_signal(barrier, inc=1, device_id=dev, device_id_type=pl.DeviceIdType.MESH)
    load_off.wait()
    load_ex.wait()
    offs = [off[0, s] for s in range(SLOTS)]
    exps = [ex[0, s] for s in range(SLOTS)]
    lane8 = lax.broadcasted_iota(jnp.int32, (8, 128), 1)
    note = jnp.zeros((8, 128), jnp.int32)
    for s in range(SLOTS):
        note = jnp.where(lane8 == s, offs[s], note)
        note = jnp.where(lane8 == 8 + s, exps[s], note)
    meta[0] = note
    pl.semaphore_wait(barrier, len(met))

    def one_tile(src, d, j, sem, dev):
        return remote(src.at[j], rb[d].at[j], ts.at[sem + j], tr.at[d, j], dev)

    mine = tv.at[0]
    own_down = [one_tile(mine, 4, j, 0, below) for j in range(6)]
    own_facing = [one_tile(mine, 2, j, 6, facing) for j in range(6)]
    on_facing = [one_tile(rb4, 2, j, 6, facing) for j in range(6)]
    on_down = [one_tile(rb2, 6, j, 12, below) for j in range(3)]
    across = [one_tile(rb4, 6, j, 15, facing) for j in range(3)]
    far_tile = remote(rb4.at[0], rb7.at[0], ts.at[18], tp.at[7, 0], at_blk(q - 2, 1))

    def both(*tests):
        keep = tests[0]
        for test in tests[1:]:
            keep = jnp.logical_and(keep, test)
        return keep

    def up_to(j, limits):
        return c >= 0 if j < limits[1] else (c == 0 if j < limits[0] else c < 0)

    def comes_down(j):
        return jnp.logical_or(even, up_to(j, SECOND))

    def part(src, d, p, sem):
        lo, hi = PARTS[d][p]
        return remote(src.at[pl.ds(lo, hi - lo)], rb[d].at[pl.ds(lo, hi - lo)], ts.at[sem + p], tp.at[d, p], sibling)

    def vectors(src, d, sem, dev):
        return remote(vs.at[src], vs.at[d], vsend.at[sem], vrecv.at[d], dev)

    v_down = vectors(0, 4, 0, below)
    v_facing = vectors(0, 2, 1, facing)
    v_on_facing = vectors(4, 2, 1, facing)
    v_on_down = vectors(2, 6, 2, below)
    v_across = vectors(4, 6, 3, facing)
    v_far = vectors(4, 7, 4, at_blk(q - 2, 1))
    v_near = vectors(0, 1, 5, sibling)
    v_hand_on = [None] + [[vectors(2 * k, d, 5 + k, sibling) for d in (2 * k - 1, 2 * k + 1)] for k in (1, 2, 3)]

    near_tiles = [part(mine, 1, p, 19) for p in range(2)]
    note_out = [
        remote(meta.at[0], meta.at[d], ms.at[d], mr.at[d], at_behind(d)) for d in range(1, REACH)
    ]
    for copy in note_out:
        copy.start()

    def by_core(copies, act):
        for core in range(2):
            if copies[core] is not None:
                @pl.when(c == core)
                def _(copy=copies[core]):
                    act(copy)

    def go(copy):
        copy.start()

    def left_here(copy):
        copy.wait_send()

    def has_come(copy):
        copy.wait_recv()

    def when(test, act, copy):
        @pl.when(test)
        def _():
            act(copy)

    for j in range(6):
        when(odd, go, own_facing[j])
        when(comes_down(j), go, own_down[j])
    load_v0.wait()
    when(odd, go, v_facing)
    v_down.start()
    when(c == 1, go, v_near)

    @pl.when(c == 1)
    def _():
        for copy in near_tiles:
            copy.start()

    def hand_on(k, p):
        return [
            part(rb[2 * k], d, p, 19 + 2 * k) if p < len(PARTS[d]) else None
            for d in (2 * k - 1, 2 * k + 1)
        ]

    def here(d):
        for p in range(len(PARTS[d])):
            part(rb[d], d, p, 19).wait_recv()

    def absorb(d, right_ref, first):
        slot = jnp.int32(0)
        grade = jnp.float32(0.0)
        for r in range(SLOTS):
            hit = offs[r] == d
            slot = jnp.where(hit, r, slot)
            grade = jnp.where(hit, power_of_two(exps[r]), grade)
        left = own[slot]

        def one(s, carry):
            wanted = smeta[0, 0, s] - d
            t = jnp.int32(0)
            scale = jnp.float32(0.0)
            for j in range(NEED[d]):
                hit = smeta[d, 0, j] == wanted
                t = jnp.where(hit, j, t)
                scale = jnp.where(hit, power_of_two(smeta[d, 0, 8 + j]), scale)
            product = jnp.dot(left, right_ref[t], preferred_element_type=F32) * (grade * scale)
            if first:
                paths[s] = product
            else:
                paths[s] = paths[s] + product
            return carry

        lax.fori_loop(0 if d == 0 else max(1, d - 2), SLOTS, one, 0)

    for j in range(6):
        when(comes_down(j), has_come, own_down[j])
        if j == 0:
            when(c == 0, go, far_tile)
        when(even, go, on_facing[j])
        if j in ACROSS:
            when(both(odd, up_to(j, THIRD)), go, across[j])
        own_facing[j].wait_recv()
        if j < 3:
            when(both(odd, up_to(j, THIRD)) if j in ACROSS else up_to(j, THIRD), go, on_down[j])
        if j == 2:
            by_core(hand_on(1, 0), go)
            by_core(hand_on(2, 0), go)
            for copy in note_out:
                copy.wait_recv()
            to_scalar = pltpu.make_async_copy(meta, smeta, smeta_sem)
            to_scalar.start()
            to_scalar.wait()
            load_own.wait()
            absorb(0, own, True)
        if j == 4:
            by_core(hand_on(2, 1), go)
    by_core(hand_on(1, 1), go)
    v_down.wait_recv()
    when(even, go, v_on_facing)
    when(odd, go, v_across)
    when(c == 0, go, v_far)
    by_core(v_hand_on[2], go)
    absorb(4, rb4, False)
    absorb(2, rb2, False)
    for j in range(3):
        when(up_to(j, THIRD), has_come, on_down[j])
    by_core(hand_on(3, 0), go)
    v_facing.wait_recv()
    when(odd, go, v_on_down)
    by_core(v_hand_on[1], go)
    absorb(6, rb6, False)
    for d in (1, 3, 5, 7):
        here(d)
        absorb(d, rb[d], False)

    v_on_down.wait_recv()
    by_core(v_hand_on[3], go)

    ones = jnp.ones((8, TILE), BF16)
    degree = jnp.zeros((8, TILE), F32)
    for s in range(SLOTS):
        tile = ((own[s].astype(F32) * power_of_two(exps[s])) * paths[s]).astype(BF16)
        motif[s] = tile
        degree = degree + lax.dot_general(ones, tile, NT, preferred_element_type=F32)
    degree = degree[0:1, :]
    root = lax.rsqrt(degree)

    def exchange(xs, ssem, rsem):
        direct = [
            remote(xs.at[0], xs.at[2 * k], ssem.at[k], rsem.at[2 * k], at_blk(q - k, c)) for k in (1, 2, 3)
        ]
        far = remote(xs.at[0], xs.at[7], ssem.at[4], rsem.at[7], cross)
        near = remote(xs.at[0], xs.at[1], ssem.at[5], rsem.at[1], sibling)
        direct[2].start()
        by_core([far, near], go)
        direct[1].start()
        direct[0].start()
        return direct

    def passing(xs, ssem, rsem, k):
        return [
            remote(xs.at[2 * k], xs.at[d], ssem.at[5 + k], rsem.at[d], sibling)
            for d in (2 * k - 1, 2 * k + 1)
        ]

    def relay(xs, ssem, rsem, direct):
        for k in (1, 2, 3):
            direct[k - 1].wait_recv()
            by_core(passing(xs, ssem, rsem, k), go)

    def rest(xs, ssem, rsem):
        for d in (1, 3, 5, 7):
            remote(xs.at[d], xs.at[d], ssem.at[0], rsem.at[d], sibling).wait_recv()

    def all_left(xs, ssem, rsem, direct):
        for copy in direct:
            copy.wait_send()
        far = remote(xs.at[0], xs.at[7], ssem.at[4], rsem.at[7], cross)
        near = remote(xs.at[0], xs.at[1], ssem.at[5], rsem.at[1], sibling)
        by_core([far, near], left_here)
        for k in (1, 2, 3):
            by_core(passing(xs, ssem, rsem, k), left_here)

    def apply_graph(xs):
        total = jnp.zeros((VEC, TILE), F32)
        for s in range(SLOTS):
            total = total + lax.dot_general(xs[offs[s]], motif[s], NT, preferred_element_type=F32)
        return total

    lane = lax.broadcasted_iota(jnp.int32, (64, 128), 1)
    row = lax.broadcasted_iota(jnp.int32, (64, 128), 0)
    left = lane < VEC
    zeros = jnp.zeros((64, 128), F32)

    def gram(i, vectors):
        both = dot32(vectors, jnp.concatenate([vectors, vectors], axis=0), NT)
        g_src[i] = jnp.where(left[:32], both[:32], both[32:]) / NODES

    def copies_b(i):
        own_half, other_half = pl.ds(c * HALF, HALF), pl.ds((1 - c) * HALF, HALF)
        return [
            remote(g_src.at[i, other_half], gb.at[i, 3 + j], gbs.at[i, 3 + j], gbr.at[i, 3 + j], x_others[j])
            for j in range(NX)
        ] + [
            remote(g_src.at[i, own_half], gb.at[i, j], gbs.at[i, j], gbr.at[i, j], x_mates[j])
            for j in range(NX - 1)
        ]

    def copies_c(i):
        return [remote(gc_src.at[i], gc.at[i, j], gcs.at[i, j], gcr.at[i, j], y_mates[j]) for j in range(NY - 1)]

    def copies_d(i):
        return [remote(gd_src.at[i], gd.at[i, j], gds.at[i, j], gdr.at[i, j], z_mates[j]) for j in range(NZ - 1)]

    def copies_e(i):
        mine = pl.ds(c * HALF, HALF)
        return [remote(fin.at[i, mine], fin.at[i, mine], ges.at[i], ger.at[i], sibling)]

    def start(copies):
        for copy in copies:
            copy.start()

    def arrive(copies):
        for copy in copies:
            copy.wait_recv()

    def step_b(i):
        start(copies_b(i))

    def step_c(i):
        arrive(copies_b(i))
        gc_src[i] = g_src[i, pl.ds(c * HALF, HALF), :] + sum(gb[i, j] for j in range(1, 7)) + gb[i, 0]
        start(copies_c(i))

    def step_d(i):
        arrive(copies_c(i))
        gd_src[i] = gc_src[i] + sum(gc[i, j] for j in range(1, 7)) + gc[i, 0]
        start(copies_d(i))

    def step_e(i):
        arrive(copies_d(i))
        fin[i, pl.ds(c * HALF, HALF), :] = gd_src[i] + sum(gd[i, j] for j in range(1, 7)) + gd[i, 0]
        start(copies_e(i))

    def collect(i):
        other = pl.ds((1 - c) * HALF, HALF)
        remote(fin.at[i, other], fin.at[i, other], ges.at[i], ger.at[i], sibling).wait_recv()
        packed = fin[i]
        turned = pltpu.roll(packed, 64, 1)
        return jnp.concatenate(
            [jnp.where(left[:32], packed, turned), jnp.where(left[:32], turned, packed)], axis=0
        )

    roots[0] = root
    root_out = [
        remote(roots.at[0], roots.at[d], rsend.at[d], rrecv.at[d], at_behind(d)) for d in (7, 6, 5, 4, 3, 2, 1)
    ]
    start(root_out)
    for d in (1, 3, 5, 7):
        vectors(0, d, 0, sibling).wait_recv()
    arrive(root_out)
    total = jnp.zeros((VEC, TILE), F32)
    for s in range(SLOTS):
        input_s = (vs[offs[s]].astype(F32) * roots[offs[s]]).astype(BF16)
        total = total + lax.dot_general(input_s, motif[s], NT, preferred_element_type=F32)
    input_1 = (vs[0].astype(F32) * root).astype(BF16).astype(F32)
    scaled_1 = (total + degree * input_1) * root

    wide_2 = scaled_1 * root
    xs2[0] = wide_2.astype(BF16)
    sent_2 = exchange(xs2, x2s, x2r)
    gram(0, scaled_1)
    step_b(0)
    relay(xs2, x2s, x2r, sent_2)
    step_c(0)
    rest(xs2, x2s, x2r)
    scaled_2 = (apply_graph(xs2) + degree * wide_2) * root
    gram(1, scaled_2)
    step_b(1)
    step_d(0)
    step_c(1)
    step_e(0)
    step_d(1)
    gram_1 = collect(0)
    augmented = jnp.where(left, gram_1, jnp.where(lane == row + VEC, 1.0, 0.0))
    blocks = eliminate([augmented[8 * i : 8 * i + 8] for i in range(8)], 0, VEC)
    inverse_1 = jnp.where(left, 0.0, finish(blocks))
    step_e(1)
    gram_2 = jnp.where(left, 0.0, collect(1))
    half_way = dot32(inverse_1, jnp.concatenate([zeros, gram_2], axis=0))
    middle = dot32(half_way, jnp.concatenate([inverse_1, zeros], axis=0), NT)
    augmented = jnp.where(left, middle, inverse_1)
    blocks = eliminate([augmented[8 * i : 8 * i + 8] for i in range(8)], 0, VEC)
    inverse_2 = jnp.where(left, 0.0, finish(blocks))
    out[...] = dot32(inverse_2, jnp.concatenate([jnp.zeros((VEC, TILE), F32), scaled_2], axis=0))

    for copy in note_out:
        copy.wait_send()
    for j in range(6):
        when(comes_down(j), left_here, own_down[j])
        own_facing[j].wait_send()
        if j < 3:
            when(both(odd, up_to(j, THIRD)) if j in ACROSS else up_to(j, THIRD), left_here, on_down[j])
        if j in ACROSS:
            when(both(odd, up_to(j, THIRD)), left_here, across[j])

    @pl.when(c == 0)
    def _():
        far_tile.wait_send()

    @pl.when(c == 1)
    def _():
        for copy in near_tiles:
            copy.wait_send()

    for copy in [v_down] + root_out:
        copy.wait_send()
    v_facing.wait_send()
    when(odd, left_here, v_across)
    when(odd, left_here, v_on_down)
    when(c == 0, left_here, v_far)
    when(c == 1, left_here, v_near)
    for k in (1, 2, 3):
        by_core(v_hand_on[k], left_here)
    all_left(xs2, x2s, x2r, sent_2)
    for k in (1, 2, 3):
        for p in range(2):
            by_core(hand_on(k, p), left_here)
    for i in range(2):
        for copies in (copies_b, copies_c, copies_d, copies_e):
            for copy in copies(i):
                copy.wait_send()


def shards(tile_values, tile_offset, tile_exponent, initial_vectors):
    dma = pltpu.SemaphoreType.DMA
    tiles = [pltpu.VMEM((ROWS[d], TILE, TILE), BF16) for d in range(1, REACH)]
    basis_t = pl.pallas_call(
        kernel,
        out_shape=jax.ShapeDtypeStruct((VEC, TILE), F32),
        in_specs=[
            pl.BlockSpec(memory_space=pltpu.HBM),
            pl.BlockSpec(memory_space=pltpu.HBM),
            pl.BlockSpec(memory_space=pltpu.HBM),
            pl.BlockSpec(memory_space=pltpu.HBM),
        ],
        out_specs=pl.BlockSpec(memory_space=pltpu.VMEM),
        scratch_shapes=[
            pltpu.VMEM((SLOTS, TILE, TILE), BF16),
            *tiles,
            pltpu.SMEM((1, SLOTS), jnp.int32),
            pltpu.SMEM((1, SLOTS), jnp.int32),
            pltpu.VMEM((REACH, 8, 128), jnp.int32),
            pltpu.SMEM((REACH, 8, 128), jnp.int32),
            pltpu.VMEM((SLOTS, TILE, TILE), F32),
            pltpu.VMEM((SLOTS, TILE, TILE), BF16),
            pltpu.VMEM((REACH, VEC, TILE), BF16),
            pltpu.VMEM((REACH, 1, TILE), F32),
            pltpu.VMEM((REACH, VEC, TILE), BF16),
            pltpu.VMEM((2, 2 * HALF, 128), F32),
            pltpu.VMEM((2, 2 * NX - 1, HALF, 128), F32),
            pltpu.VMEM((2, HALF, 128), F32),
            pltpu.VMEM((2, NY - 1, HALF, 128), F32),
            pltpu.VMEM((2, HALF, 128), F32),
            pltpu.VMEM((2, NZ - 1, HALF, 128), F32),
            pltpu.VMEM((2, 2 * HALF, 128), F32),
            dma, dma((3,)), dma,
            dma((27,)), dma((8, 6)), dma((8, 2)),
            dma((8,)), dma((8,)),
            dma((9,)), dma((8,)),
            dma((8,)), dma((8,)),
            dma((9,)), dma((8,)),
            dma((2, 2 * NX - 1)), dma((2, 2 * NX - 1)),
            dma((2, NY - 1)), dma((2, NY - 1)),
            dma((2, NZ - 1)), dma((2, NZ - 1)),
            dma((2,)), dma((2,)),
        ],
        compiler_params=pltpu.CompilerParams(
            collective_id=0, has_side_effects=True, vmem_limit_bytes=55000 * 1024
        ),
        cost_estimate=pl.CostEstimate(flops=1200000000, bytes_accessed=1000000, transcendentals=0),
        name="embed",
    )(tile_values, tile_offset, tile_exponent, initial_vectors.T)
    return basis_t.T


def solution(mesh):
    return jax.shard_map(
        shards,
        mesh=mesh,
        in_specs=(
            P(("grp", "blk"), None, None, None),
            P(("grp", "blk"), None),
            P(("grp", "blk"), None),
            P(("grp", "blk"), None),
        ),
        out_specs=P(("grp", "blk"), None),
        check_vma=False,
    )
```

```python
import jax
import jax.numpy as jnp
from jax import lax
from jax.experimental import pallas as pl
from jax.experimental.pallas import tpu as pltpu
from jax.sharding import PartitionSpec as P

TILE = 256
VEC = 64
SLOTS = 6
REACH = 8
NODES = 131072
BLK = 32
CHIPS = 16
NX, NY, NZ = 4, 8, 8
RING = (4, 3, 5, 2, 6, 1, 7)
HALF = 16
F32 = jnp.float32
BF16 = jnp.bfloat16
NEED = [min(SLOTS, REACH - d) for d in range(REACH)]
SECOND = [5, 4]
THIRD = [3, 2]
ACROSS = (1, 2)
PARTS = {1: [(0, 3), (3, 5), (5, 6)], 3: [(0, 3), (3, 5)], 5: [(0, 3)], 7: [(0, 1)]}
ROWS = {1: 6, 2: 6, 3: 5, 4: 6, 5: 3, 6: 3, 7: 1}
NT = (((1,), (1,)), ((), ()))


def power_of_two(e):
    one = jnp.float32(1.0)
    return jnp.where(
        e == -2, 0.25 * one,
        jnp.where(e == -1, 0.5 * one, jnp.where(e == 0, one, jnp.where(e == 1, 2 * one, 4 * one))),
    )


def dot32(a, b, dims=(((1,), (0,)), ((), ()))):
    return lax.dot_general(
        a, b, dims, precision=lax.Precision.HIGHEST, preferred_element_type=F32
    )


def reciprocal(x):
    guess = pl.reciprocal(x, approx=True)
    guess = guess * (2.0 - x * guess)
    return guess * (2.0 - x * guess)


def eliminate(blocks, first, last):
    blocks = list(blocks)
    sub = lax.broadcasted_iota(jnp.int32, (8, 128), 0)

    def spread(row):
        return jnp.broadcast_to(row, (8, 128))

    for k in range(first, last, 4):
        kb, kr = divmod(k, 8)
        head = blocks[kb]
        columns = {
            i: [spread(blocks[i][:, k + j : k + j + 1]) for j in range(4)]
            for i in range(kb, 8)
        }
        upper = [spread(head[kr + j : kr + j + 1, :]) for j in range(4)]
        corner = [[spread(columns[kb][j][kr + a : kr + a + 1, :]) for j in range(4)] for a in range(4)]
        inverse = []
        for a in (0, 2):
            inverse.append(reciprocal(corner[a][a]))
            low = corner[a][a + 1] * inverse[a]
            minor = corner[a][a] * corner[a + 1][a + 1] - corner[a][a + 1] * corner[a][a + 1]
            inverse.append(corner[a][a] * reciprocal(minor))
            for j in range(a + 1, 4):
                corner[a + 1][j] = corner[a + 1][j] - low * corner[a][j]
            upper[a + 1] = upper[a + 1] - low * upper[a]
            for r in range(a + 2, 4):
                for e in (a, a + 1):
                    low = corner[e][r] * inverse[e]
                    for j in range(r, 4):
                        corner[r][j] = corner[r][j] - low * corner[e][j]
                    upper[r] = upper[r] - low * upper[e]
        for i in range(kb, 8):
            if i == kb and kr == 4:
                continue
            block = blocks[i]
            factors = []
            for a in range(4):
                rest = columns[i][a]
                for e in range(a):
                    rest = rest - factors[e] * corner[e][a]
                factors.append(rest * inverse[a])
            for a in range(4):
                block = block - factors[a] * upper[a]
            blocks[i] = block if i > kb else jnp.where(sub > kr + 3, block, head)
        done = blocks[kb]
        for a in range(4):
            done = jnp.where(sub == kr + a, upper[a], done)
        blocks[kb] = done
    return blocks


def finish(blocks):
    lane = lax.broadcasted_iota(jnp.int32, (8, 128), 1)
    sub = lax.broadcasted_iota(jnp.int32, (8, 128), 0)
    done = []
    for i, block in enumerate(blocks):
        pivot = jnp.sum(jnp.where(lane == sub + 8 * i, block, 0.0), axis=1, keepdims=True)
        done.append(block * lax.rsqrt(pivot))
    return jnp.concatenate(done, axis=0)


def kernel(
    tv, off_any, ex_any, v0, out,
    own, rb1, rb2, rb3, rb4, rb5, rb6, rb7, off, ex, meta, smeta, paths, motif, vs, roots, xs2,
    g_src, gb, gc_src, gc, gd_src, gd, fin,
    own_sem, in_sem, smeta_sem, ts, tr, tp, ms, mr, vsend, vrecv, rsend, rrecv, x2s, x2r,
    gbs, gbr, gcs, gcr, gds, gdr, ges, ger,
):
    rb = {1: rb1, 2: rb2, 3: rb3, 4: rb4, 5: rb5, 6: rb6, 7: rb7}
    g = lax.axis_index("grp")
    b = lax.axis_index("blk")
    c = lax.rem(b, 2)
    q = b // 2
    x_hi, z = lax.rem(q, 2), q // 2
    x_lo, y = lax.rem(g, 2), g // 2
    x = x_hi * 2 + x_lo

    def at_blk(chip, core):
        return {"grp": g, "blk": lax.rem(chip + 2 * CHIPS, CHIPS) * 2 + core}

    def at_behind(d):
        return {"grp": g, "blk": lax.rem(b + BLK - d, BLK)}

    def at_xyz(xx, yy, zz, core=c):
        return {
            "grp": yy * 2 + lax.rem(xx, 2),
            "blk": (zz * 2 + xx // 2) * 2 + core,
        }

    sibling = at_blk(q, 1 - c)
    cross = at_blk(q - 4 + 8 * c, 1 - c)
    facing = at_blk(q + 1 - 2 * x_hi, c)
    even, odd = x_hi == 0, x_hi == 1
    below = at_blk(q - 2, c)
    x_mates = [at_xyz(lax.rem(x + j, NX), y, z) for j in (2, 1, 3)]
    x_others = [at_xyz(lax.rem(x + j, NX), y, z, 1 - c) for j in (2, 1, 3, 0)]
    y_mates = [at_xyz(x, lax.rem(y + j, NY), z) for j in RING]
    z_mates = [at_xyz(x, y, lax.rem(z + j, NZ)) for j in RING]

    def remote(src, dst, ssem, rsem, dev):
        return pltpu.make_async_remote_copy(
            src_ref=src, dst_ref=dst, send_sem=ssem, recv_sem=rsem,
            device_id=dev, device_id_type=pl.DeviceIdType.MESH,
        )

    load_own = pltpu.make_async_copy(tv.at[0], own, own_sem)
    load_own.start()
    load_off = pltpu.make_async_copy(off_any, off, in_sem.at[0])
    load_ex = pltpu.make_async_copy(ex_any, ex, in_sem.at[1])
    load_off.start()
    load_ex.start()
    load_v0 = pltpu.make_async_copy(v0, vs.at[0], in_sem.at[2])
    load_v0.start()

    barrier = pltpu.get_barrier_semaphore()
    met = y_mates + z_mates[:5] + x_mates[1:] + x_others[1:3]
    for d in range(REACH - 1, 0, -1):
        met.append(at_behind(d))
        met.append(at_behind(-d))
    for dev in met:
        pl.semaphore_signal(barrier, inc=1, device_id=dev, device_id_type=pl.DeviceIdType.MESH)
    load_off.wait()
    load_ex.wait()
    offs = [off[0, s] for s in range(SLOTS)]
    exps = [ex[0, s] for s in range(SLOTS)]
    lane8 = lax.broadcasted_iota(jnp.int32, (8, 128), 1)
    note = jnp.zeros((8, 128), jnp.int32)
    for s in range(SLOTS):
        note = jnp.where(lane8 == s, offs[s], note)
        note = jnp.where(lane8 == 8 + s, exps[s], note)
    meta[0] = note
    pl.semaphore_wait(barrier, len(met))

    def one_tile(src, d, j, sem, dev):
        return remote(src.at[j], rb[d].at[j], ts.at[sem + j], tr.at[d, j], dev)

    mine = tv.at[0]
    own_down = [one_tile(mine, 4, j, 0, below) for j in range(6)]
    own_facing = [one_tile(mine, 2, j, 6, facing) for j in range(6)]
    on_facing = [one_tile(rb4, 2, j, 6, facing) for j in range(6)]
    on_down = [one_tile(rb2, 6, j, 12, below) for j in range(3)]
    across = [one_tile(rb4, 6, j, 15, facing) for j in range(3)]
    far_tile = remote(rb4.at[0], rb7.at[0], ts.at[18], tp.at[7, 0], at_blk(q - 2, 1))

    def both(*tests):
        keep = tests[0]
        for test in tests[1:]:
            keep = jnp.logical_and(keep, test)
        return keep

    def up_to(j, limits):
        return c >= 0 if j < limits[1] else (c == 0 if j < limits[0] else c < 0)

    def comes_down(j):
        return jnp.logical_or(even, up_to(j, SECOND))

    def part(src, d, p, sem):
        lo, hi = PARTS[d][p]
        return remote(src.at[pl.ds(lo, hi - lo)], rb[d].at[pl.ds(lo, hi - lo)], ts.at[sem + p], tp.at[d, p], sibling)

    def vectors(src, d, sem, dev):
        return remote(vs.at[src], vs.at[d], vsend.at[sem], vrecv.at[d], dev)

    v_down = vectors(0, 4, 0, below)
    v_facing = vectors(0, 2, 1, facing)
    v_on_facing = vectors(4, 2, 1, facing)
    v_on_down = vectors(2, 6, 2, below)
    v_across = vectors(4, 6, 3, facing)
    v_far = vectors(4, 7, 4, at_blk(q - 2, 1))
    v_near = vectors(0, 1, 5, sibling)
    v_hand_on = [None] + [[vectors(2 * k, d, 5 + k, sibling) for d in (2 * k - 1, 2 * k + 1)] for k in (1, 2, 3)]

    near_tiles = [part(mine, 1, p, 19) for p in range(3)]
    note_out = [
        remote(meta.at[0], meta.at[d], ms.at[d], mr.at[d], at_behind(d)) for d in range(REACH - 1, 0, -1)
    ]
    def by_core(copies, act):
        for core in range(2):
            if copies[core] is not None:
                @pl.when(c == core)
                def _(copy=copies[core]):
                    act(copy)

    def go(copy):
        copy.start()

    def left_here(copy):
        copy.wait_send()

    def has_come(copy):
        copy.wait_recv()

    def when(test, act, copy):
        @pl.when(test)
        def _():
            act(copy)

    for copy in note_out:
        copy.start()
    for j in range(SLOTS):
        when(odd, go, own_facing[j])
        when(comes_down(j), go, own_down[j])
    load_v0.wait()
    when(odd, go, v_facing)
    v_down.start()
    when(c == 1, go, v_near)

    @pl.when(c == 1)
    def _():
        for copy in near_tiles:
            copy.start()

    def hand_on(k, p):
        return [
            part(rb[2 * k], d, p, 19 + 3 * k) if p < len(PARTS[d]) else None
            for d in (2 * k - 1, 2 * k + 1)
        ]

    def here(d):
        for p in range(len(PARTS[d])):
            part(rb[d], d, p, 19).wait_recv()

    def absorb(d, right_ref, first):
        slot = jnp.int32(0)
        grade = jnp.float32(0.0)
        for r in range(SLOTS):
            hit = offs[r] == d
            slot = jnp.where(hit, r, slot)
            grade = jnp.where(hit, power_of_two(exps[r]), grade)
        left = own[slot]

        def one(s, carry):
            wanted = smeta[0, 0, s] - d
            t = jnp.int32(0)
            scale = jnp.float32(0.0)
            for j in range(NEED[d]):
                hit = smeta[d, 0, j] == wanted
                t = jnp.where(hit, j, t)
                scale = jnp.where(hit, power_of_two(smeta[d, 0, 8 + j]), scale)
            product = jnp.dot(left, right_ref[t], preferred_element_type=F32) * (grade * scale)
            if first:
                paths[s] = product
            else:
                paths[s] = paths[s] + product
            return carry

        lax.fori_loop(0 if d == 0 else max(1, d - 2), SLOTS, one, 0, unroll=True)

    for j in range(6):
        when(comes_down(j), has_come, own_down[j])
        if j == 0:
            when(c == 0, go, far_tile)
        when(even, go, on_facing[j])
        if j in ACROSS:
            when(both(odd, up_to(j, THIRD)), go, across[j])
        own_facing[j].wait_recv()
        if j < 3:
            when(both(odd, up_to(j, THIRD)) if j in ACROSS else up_to(j, THIRD), go, on_down[j])
        if j == 2:
            by_core(hand_on(1, 0), go)
            by_core(hand_on(2, 0), go)
            for copy in note_out:
                copy.wait_recv()
            to_scalar = pltpu.make_async_copy(meta, smeta, smeta_sem)
            to_scalar.start()
            to_scalar.wait()
            load_own.wait()
            absorb(0, own, True)
        if j == 4:
            by_core(hand_on(1, 1), go)
            by_core(hand_on(2, 1), go)
    by_core(hand_on(1, 2), go)
    v_down.wait_recv()
    when(even, go, v_on_facing)
    when(odd, go, v_across)
    when(c == 0, go, v_far)
    by_core(v_hand_on[2], go)
    absorb(4, rb4, False)
    absorb(2, rb2, False)
    for j in range(3):
        when(up_to(j, THIRD), has_come, on_down[j])
    by_core(hand_on(3, 0), go)
    v_facing.wait_recv()
    when(odd, go, v_on_down)
    by_core(v_hand_on[1], go)
    absorb(6, rb6, False)
    for d in (1, 3, 5, 7):
        here(d)
        absorb(d, rb[d], False)

    v_on_down.wait_recv()
    by_core(v_hand_on[3], go)

    ones = jnp.ones((8, TILE), BF16)
    degree = jnp.zeros((8, TILE), F32)
    for s in range(SLOTS):
        tile = ((own[s].astype(F32) * power_of_two(exps[s])) * paths[s]).astype(BF16)
        motif[s] = tile
        degree = degree + lax.dot_general(ones, tile, NT, preferred_element_type=F32)
    degree = degree[0:1, :]
    root = lax.rsqrt(degree)

    def exchange(xs, ssem, rsem):
        direct = [
            remote(xs.at[0], xs.at[2 * k], ssem.at[k], rsem.at[2 * k], at_blk(q - k, c)) for k in (1, 2, 3)
        ]
        far = remote(xs.at[0], xs.at[7], ssem.at[4], rsem.at[7], cross)
        near = remote(xs.at[0], xs.at[1], ssem.at[5], rsem.at[1], sibling)
        direct[2].start()
        by_core([far, near], go)
        direct[1].start()
        direct[0].start()
        return direct

    def passing(xs, ssem, rsem, k):
        return [
            remote(xs.at[2 * k], xs.at[d], ssem.at[5 + k], rsem.at[d], sibling)
            for d in (2 * k - 1, 2 * k + 1)
        ]

    def relay(xs, ssem, rsem, direct):
        for k in (1, 2, 3):
            direct[k - 1].wait_recv()
            by_core(passing(xs, ssem, rsem, k), go)

    def rest(xs, ssem, rsem):
        for d in (1, 3, 5, 7):
            remote(xs.at[d], xs.at[d], ssem.at[0], rsem.at[d], sibling).wait_recv()

    def all_left(xs, ssem, rsem, direct):
        for copy in direct:
            copy.wait_send()
        far = remote(xs.at[0], xs.at[7], ssem.at[4], rsem.at[7], cross)
        near = remote(xs.at[0], xs.at[1], ssem.at[5], rsem.at[1], sibling)
        by_core([far, near], left_here)
        for k in (1, 2, 3):
            by_core(passing(xs, ssem, rsem, k), left_here)

    def apply_graph(xs):
        total = jnp.zeros((VEC, TILE), F32)
        for s in range(SLOTS):
            total = total + lax.dot_general(xs[offs[s]], motif[s], NT, preferred_element_type=F32)
        return total

    lane = lax.broadcasted_iota(jnp.int32, (64, 128), 1)
    row = lax.broadcasted_iota(jnp.int32, (64, 128), 0)
    left = lane < VEC
    zeros = jnp.zeros((64, 128), F32)

    def gram(i, vectors):
        both = dot32(vectors, jnp.concatenate([vectors, vectors], axis=0), NT)
        g_src[i] = jnp.where(left[:32], both[:32], both[32:]) / NODES

    def copies_b(i):
        own_half, other_half = pl.ds(c * HALF, HALF), pl.ds((1 - c) * HALF, HALF)
        copies = []
        for j in range(NX):
            copies.append(remote(g_src.at[i, other_half], gb.at[i, j], gbs.at[i, j], gbr.at[i, j], x_others[j]))
            if j < NX - 1:
                n = NX + j
                copies.append(remote(g_src.at[i, own_half], gb.at[i, n], gbs.at[i, n], gbr.at[i, n], x_mates[j]))
        return copies

    def copies_c(i):
        return [remote(gc_src.at[i], gc.at[i, j], gcs.at[i, j], gcr.at[i, j], y_mates[j]) for j in range(NY - 1)]

    def copies_d(i):
        return [remote(gd_src.at[i], gd.at[i, j], gds.at[i, j], gdr.at[i, j], z_mates[j]) for j in range(NZ - 1)]

    def copies_e(i):
        mine = pl.ds(c * HALF, HALF)
        return [remote(fin.at[i, mine], fin.at[i, mine], ges.at[i], ger.at[i], sibling)]

    def start(copies):
        for copy in copies:
            copy.start()

    def arrive(copies):
        for copy in copies:
            copy.wait_recv()

    def step_b(i):
        start(copies_b(i))

    def step_c(i):
        arrive(copies_b(i))
        gc_src[i] = g_src[i, pl.ds(c * HALF, HALF), :] + sum(gb[i, j] for j in range(1, 7)) + gb[i, 0]
        start(copies_c(i))

    def step_d(i):
        arrive(copies_c(i))
        gd_src[i] = gc_src[i] + sum(gc[i, j] for j in range(1, 7)) + gc[i, 0]
        start(copies_d(i))

    def step_e(i):
        arrive(copies_d(i))
        fin[i, pl.ds(c * HALF, HALF), :] = gd_src[i] + sum(gd[i, j] for j in range(1, 7)) + gd[i, 0]
        start(copies_e(i))

    def collect(i):
        other = pl.ds((1 - c) * HALF, HALF)
        remote(fin.at[i, other], fin.at[i, other], ges.at[i], ger.at[i], sibling).wait_recv()
        packed = fin[i]
        turned = pltpu.roll(packed, 64, 1)
        return jnp.concatenate(
            [jnp.where(left[:32], packed, turned), jnp.where(left[:32], turned, packed)], axis=0
        )

    roots[0] = root
    root_out = [
        remote(roots.at[0], roots.at[d], rsend.at[d], rrecv.at[d], at_behind(d)) for d in (7, 6, 5, 4, 3, 2, 1)
    ]
    start(root_out)
    for d in (1, 3, 5, 7):
        vectors(0, d, 0, sibling).wait_recv()
    arrive(root_out)
    total = jnp.zeros((VEC, TILE), F32)
    for s in range(SLOTS):
        input_s = (vs[offs[s]].astype(F32) * roots[offs[s]]).astype(BF16)
        total = total + lax.dot_general(input_s, motif[s], NT, preferred_element_type=F32)
    input_1 = (vs[0].astype(F32) * root).astype(BF16).astype(F32)
    scaled_1 = (total + degree * input_1) * root

    wide_2 = scaled_1 * root
    xs2[0] = wide_2.astype(BF16)
    sent_2 = exchange(xs2, x2s, x2r)
    gram(0, scaled_1)
    step_b(0)
    relay(xs2, x2s, x2r, sent_2)
    step_c(0)
    rest(xs2, x2s, x2r)
    scaled_2 = (apply_graph(xs2) + degree * wide_2) * root
    gram(1, scaled_2)
    step_b(1)
    step_d(0)
    step_c(1)
    step_e(0)
    step_d(1)
    gram_1 = collect(0)
    augmented = jnp.where(left, gram_1, jnp.where(lane == row + VEC, 1.0, 0.0))
    blocks = eliminate([augmented[8 * i : 8 * i + 8] for i in range(8)], 0, VEC)
    inverse_1 = jnp.where(left, 0.0, finish(blocks))
    step_e(1)
    gram_2 = jnp.where(left, 0.0, collect(1))
    half_way = dot32(inverse_1, jnp.concatenate([zeros, gram_2], axis=0))
    middle = dot32(half_way, jnp.concatenate([inverse_1, zeros], axis=0), NT)
    augmented = jnp.where(left, middle, inverse_1)
    blocks = eliminate([augmented[8 * i : 8 * i + 8] for i in range(8)], 0, VEC)
    inverse_2 = jnp.where(left, 0.0, finish(blocks))
    out[...] = dot32(inverse_2, jnp.concatenate([jnp.zeros((VEC, TILE), F32), scaled_2], axis=0))

    for copy in note_out:
        copy.wait_send()
    for j in range(6):
        when(comes_down(j), left_here, own_down[j])
        own_facing[j].wait_send()
        if j < 3:
            when(both(odd, up_to(j, THIRD)) if j in ACROSS else up_to(j, THIRD), left_here, on_down[j])
        if j in ACROSS:
            when(both(odd, up_to(j, THIRD)), left_here, across[j])

    @pl.when(c == 0)
    def _():
        far_tile.wait_send()

    @pl.when(c == 1)
    def _():
        for copy in near_tiles:
            copy.wait_send()

    for copy in [v_down] + root_out:
        copy.wait_send()
    v_facing.wait_send()
    when(odd, left_here, v_across)
    when(odd, left_here, v_on_down)
    when(c == 0, left_here, v_far)
    when(c == 1, left_here, v_near)
    for k in (1, 2, 3):
        by_core(v_hand_on[k], left_here)
    all_left(xs2, x2s, x2r, sent_2)
    for k in (1, 2, 3):
        for p in range(3):
            by_core(hand_on(k, p), left_here)
    for i in range(2):
        for copies in (copies_b, copies_c, copies_d, copies_e):
            for copy in copies(i):
                copy.wait_send()


def shards(tile_values, tile_offset, tile_exponent, initial_vectors):
    dma = pltpu.SemaphoreType.DMA
    tiles = [pltpu.VMEM((ROWS[d], TILE, TILE), BF16) for d in range(1, REACH)]
    basis_t = pl.pallas_call(
        kernel,
        out_shape=jax.ShapeDtypeStruct((VEC, TILE), F32),
        in_specs=[
            pl.BlockSpec(memory_space=pltpu.HBM),
            pl.BlockSpec(memory_space=pltpu.HBM),
            pl.BlockSpec(memory_space=pltpu.HBM),
            pl.BlockSpec(memory_space=pltpu.HBM),
        ],
        out_specs=pl.BlockSpec(memory_space=pltpu.VMEM),
        scratch_shapes=[
            pltpu.VMEM((SLOTS, TILE, TILE), BF16),
            *tiles,
            pltpu.SMEM((1, SLOTS), jnp.int32),
            pltpu.SMEM((1, SLOTS), jnp.int32),
            pltpu.VMEM((REACH, 8, 128), jnp.int32),
            pltpu.SMEM((REACH, 8, 128), jnp.int32),
            pltpu.VMEM((SLOTS, TILE, TILE), F32),
            pltpu.VMEM((SLOTS, TILE, TILE), BF16),
            pltpu.VMEM((REACH, VEC, TILE), BF16),
            pltpu.VMEM((REACH, 1, TILE), F32),
            pltpu.VMEM((REACH, VEC, TILE), BF16),
            pltpu.VMEM((2, 2 * HALF, 128), F32),
            pltpu.VMEM((2, 2 * NX - 1, HALF, 128), F32),
            pltpu.VMEM((2, HALF, 128), F32),
            pltpu.VMEM((2, NY - 1, HALF, 128), F32),
            pltpu.VMEM((2, HALF, 128), F32),
            pltpu.VMEM((2, NZ - 1, HALF, 128), F32),
            pltpu.VMEM((2, 2 * HALF, 128), F32),
            dma, dma((3,)), dma,
            dma((31,)), dma((8, 6)), dma((8, 3)),
            dma((8,)), dma((8,)),
            dma((9,)), dma((8,)),
            dma((8,)), dma((8,)),
            dma((9,)), dma((8,)),
            dma((2, 2 * NX - 1)), dma((2, 2 * NX - 1)),
            dma((2, NY - 1)), dma((2, NY - 1)),
            dma((2, NZ - 1)), dma((2, NZ - 1)),
            dma((2,)), dma((2,)),
        ],
        compiler_params=pltpu.CompilerParams(
            collective_id=0, has_side_effects=True, vmem_limit_bytes=55000 * 1024
        ),
        cost_estimate=pl.CostEstimate(flops=1200000000, bytes_accessed=1000000, transcendentals=0),
        name="embed",
    )(tile_values, tile_offset, tile_exponent, initial_vectors.T)
    return basis_t.T


def solution(mesh):
    return jax.shard_map(
        shards,
        mesh=mesh,
        in_specs=(
            P(("grp", "blk"), None, None, None),
            P(("grp", "blk"), None),
            P(("grp", "blk"), None),
            P(("grp", "blk"), None),
        ),
        out_specs=P(("grp", "blk"), None),
        check_vma=False,
    )
```

```python
import jax
import jax.numpy as jnp
from jax import lax
from jax.experimental import pallas as pl
from jax.experimental.pallas import tpu as pltpu
from jax.sharding import PartitionSpec as P

TILE = 256
VEC = 64
SLOTS = 6
REACH = 8
NODES = 131072
BLK = 32
CHIPS = 16
NX, NY, NZ = 4, 8, 8
RING = (4, 3, 5, 2, 6, 1, 7)
HALF = 16
F32 = jnp.float32
BF16 = jnp.bfloat16
NEED = [min(SLOTS, REACH - d) for d in range(REACH)]
SECOND = [5, 4]
THIRD = [3, 2]
ACROSS = (1, 2)
PARTS = {1: [(0, 3), (3, 5), (5, 6)], 3: [(0, 3), (3, 5)], 5: [(0, 3)], 7: [(0, 1)]}
ROWS = {1: 6, 2: 6, 3: 5, 4: 6, 5: 3, 6: 3, 7: 1}
NT = (((1,), (1,)), ((), ()))


def power_of_two(e):
    one = jnp.float32(1.0)
    return jnp.where(
        e == -2, 0.25 * one,
        jnp.where(e == -1, 0.5 * one, jnp.where(e == 0, one, jnp.where(e == 1, 2 * one, 4 * one))),
    )


def dot32(a, b, dims=(((1,), (0,)), ((), ()))):
    return lax.dot_general(
        a, b, dims, precision=lax.Precision.HIGHEST, preferred_element_type=F32
    )


def reciprocal(x):
    guess = pl.reciprocal(x, approx=True)
    guess = guess * (2.0 - x * guess)
    return guess * (2.0 - x * guess)


def eliminate(blocks, first, last):
    blocks = list(blocks)
    sub = lax.broadcasted_iota(jnp.int32, (8, 128), 0)

    def spread(row):
        return jnp.broadcast_to(row, (8, 128))

    for k in range(first, last, 4):
        kb, kr = divmod(k, 8)
        head = blocks[kb]
        columns = {
            i: [spread(blocks[i][:, k + j : k + j + 1]) for j in range(4)]
            for i in range(kb, 8)
        }
        upper = [spread(head[kr + j : kr + j + 1, :]) for j in range(4)]
        corner = [[spread(columns[kb][j][kr + a : kr + a + 1, :]) for j in range(4)] for a in range(4)]
        inverse = []
        for a in (0, 2):
            inverse.append(reciprocal(corner[a][a]))
            low = corner[a][a + 1] * inverse[a]
            minor = corner[a][a] * corner[a + 1][a + 1] - corner[a][a + 1] * corner[a][a + 1]
            inverse.append(corner[a][a] * reciprocal(minor))
            for j in range(a + 1, 4):
                corner[a + 1][j] = corner[a + 1][j] - low * corner[a][j]
            upper[a + 1] = upper[a + 1] - low * upper[a]
            for r in range(a + 2, 4):
                for e in (a, a + 1):
                    low = corner[e][r] * inverse[e]
                    for j in range(r, 4):
                        corner[r][j] = corner[r][j] - low * corner[e][j]
                    upper[r] = upper[r] - low * upper[e]
        for i in range(kb, 8):
            if i == kb and kr == 4:
                continue
            block = blocks[i]
            factors = []
            for a in range(4):
                rest = columns[i][a]
                for e in range(a):
                    rest = rest - factors[e] * corner[e][a]
                factors.append(rest * inverse[a])
            for a in range(4):
                block = block - factors[a] * upper[a]
            blocks[i] = block if i > kb else jnp.where(sub > kr + 3, block, head)
        done = blocks[kb]
        for a in range(4):
            done = jnp.where(sub == kr + a, upper[a], done)
        blocks[kb] = done
    return blocks


def finish(blocks):
    lane = lax.broadcasted_iota(jnp.int32, (8, 128), 1)
    sub = lax.broadcasted_iota(jnp.int32, (8, 128), 0)
    done = []
    for i, block in enumerate(blocks):
        pivot = jnp.sum(jnp.where(lane == sub + 8 * i, block, 0.0), axis=1, keepdims=True)
        done.append(block * lax.rsqrt(pivot))
    return jnp.concatenate(done, axis=0)


def kernel(
    tv, off_any, ex_any, v0, out,
    own, rb1, rb2, rb3, rb4, rb5, rb6, rb7, off, ex, meta, smeta, paths, motif, vs, roots, xs2,
    g_src, gb, gc_src, gc, gd_src, gd, fin,
    own_sem, in_sem, smeta_sem, ts, tr, tp, ms, mr, vsend, vrecv, rsend, rrecv, x2s, x2r,
    gbs, gbr, gcs, gcr, gds, gdr, ges, ger,
):
    rb = {1: rb1, 2: rb2, 3: rb3, 4: rb4, 5: rb5, 6: rb6, 7: rb7}
    g = lax.axis_index("grp")
    b = lax.axis_index("blk")
    c = lax.rem(b, 2)
    q = b // 2
    x_hi, z = lax.rem(q, 2), q // 2
    x_lo, y = lax.rem(g, 2), g // 2
    x = x_hi * 2 + x_lo

    def at_blk(chip, core):
        return {"grp": g, "blk": lax.rem(chip + 2 * CHIPS, CHIPS) * 2 + core}

    def at_behind(d):
        return {"grp": g, "blk": lax.rem(b + BLK - d, BLK)}

    def at_xyz(xx, yy, zz, core=c):
        return {
            "grp": yy * 2 + lax.rem(xx, 2),
            "blk": (zz * 2 + xx // 2) * 2 + core,
        }

    sibling = at_blk(q, 1 - c)
    cross = at_blk(q - 4 + 8 * c, 1 - c)
    facing = at_blk(q + 1 - 2 * x_hi, c)
    even, odd = x_hi == 0, x_hi == 1
    below = at_blk(q - 2, c)
    x_mates = [at_xyz(lax.rem(x + j, NX), y, z) for j in (2, 1, 3)]
    x_others = [at_xyz(lax.rem(x + j, NX), y, z, 1 - c) for j in (2, 1, 3, 0)]
    y_mates = [at_xyz(x, lax.rem(y + j, NY), z) for j in RING]
    z_mates = [at_xyz(x, y, lax.rem(z + j, NZ)) for j in RING]

    def remote(src, dst, ssem, rsem, dev):
        return pltpu.make_async_remote_copy(
            src_ref=src, dst_ref=dst, send_sem=ssem, recv_sem=rsem,
            device_id=dev, device_id_type=pl.DeviceIdType.MESH,
        )

    load_own = pltpu.make_async_copy(tv.at[0], own, own_sem)
    load_own.start()
    load_off = pltpu.make_async_copy(off_any, off, in_sem.at[0])
    load_ex = pltpu.make_async_copy(ex_any, ex, in_sem.at[1])
    load_off.start()
    load_ex.start()
    load_v0 = pltpu.make_async_copy(v0, vs.at[0], in_sem.at[2])
    load_v0.start()

    barrier = pltpu.get_barrier_semaphore()
    met = y_mates + z_mates[:5] + x_mates[1:] + x_others[1:3]
    for d in range(REACH - 1, 0, -1):
        met.append(at_behind(d))
        met.append(at_behind(-d))
    for dev in met:
        pl.semaphore_signal(barrier, inc=1, device_id=dev, device_id_type=pl.DeviceIdType.MESH)
    load_off.wait()
    load_ex.wait()
    offs = [off[0, s] for s in range(SLOTS)]
    exps = [ex[0, s] for s in range(SLOTS)]
    lane8 = lax.broadcasted_iota(jnp.int32, (8, 128), 1)
    note = jnp.zeros((8, 128), jnp.int32)
    for s in range(SLOTS):
        note = jnp.where(lane8 == s, offs[s], note)
        note = jnp.where(lane8 == 8 + s, exps[s], note)
    meta[0] = note
    pl.semaphore_wait(barrier, len(met))

    def one_tile(src, d, j, sem, dev):
        return remote(src.at[j], rb[d].at[j], ts.at[sem + j], tr.at[d, j], dev)

    mine = tv.at[0]
    own_down = [one_tile(mine, 4, j, 0, below) for j in range(6)]
    own_facing = [one_tile(mine, 2, j, 6, facing) for j in range(6)]
    on_facing = [one_tile(rb4, 2, j, 6, facing) for j in range(6)]
    on_down = [one_tile(rb2, 6, j, 12, below) for j in range(3)]
    across = [one_tile(rb4, 6, j, 15, facing) for j in range(3)]
    far_tile = remote(rb4.at[0], rb7.at[0], ts.at[18], tp.at[7, 0], at_blk(q - 2, 1))

    def both(*tests):
        keep = tests[0]
        for test in tests[1:]:
            keep = jnp.logical_and(keep, test)
        return keep

    def up_to(j, limits):
        return c >= 0 if j < limits[1] else (c == 0 if j < limits[0] else c < 0)

    def comes_down(j):
        return jnp.logical_or(even, up_to(j, SECOND))

    def part(src, d, p, sem):
        lo, hi = PARTS[d][p]
        return remote(src.at[pl.ds(lo, hi - lo)], rb[d].at[pl.ds(lo, hi - lo)], ts.at[sem + p], tp.at[d, p], sibling)

    def vectors(src, d, sem, dev):
        return remote(vs.at[src], vs.at[d], vsend.at[sem], vrecv.at[d], dev)

    v_down = vectors(0, 4, 0, below)
    v_facing = vectors(0, 2, 1, at_blk(q - 1, c))
    v_on_down = vectors(0, 6, 2, at_blk(q - 3, c))
    v_far = vectors(0, 7, 4, cross)
    v_near = vectors(0, 1, 5, sibling)
    v_hand_on = [None] + [[vectors(2 * k, d, 5 + k, sibling) for d in (2 * k - 1, 2 * k + 1)] for k in (1, 2, 3)]

    near_tiles = [part(mine, 1, p, 19) for p in range(3)]
    note_out = [
        remote(meta.at[0], meta.at[d], ms.at[d], mr.at[d], at_behind(d)) for d in range(REACH - 1, 0, -1)
    ]
    def by_core(copies, act):
        for core in range(2):
            if copies[core] is not None:
                @pl.when(c == core)
                def _(copy=copies[core]):
                    act(copy)

    def go(copy):
        copy.start()

    def left_here(copy):
        copy.wait_send()

    def has_come(copy):
        copy.wait_recv()

    def when(test, act, copy):
        @pl.when(test)
        def _():
            act(copy)

    for copy in note_out:
        copy.start()
    for j in range(SLOTS):
        when(odd, go, own_facing[j])
        when(comes_down(j), go, own_down[j])
    load_v0.wait()
    when(c == 1, go, v_near)

    @pl.when(c == 1)
    def _():
        for copy in near_tiles:
            copy.start()

    def hand_on(k, p):
        return [
            part(rb[2 * k], d, p, 19 + 3 * k) if p < len(PARTS[d]) else None
            for d in (2 * k - 1, 2 * k + 1)
        ]

    def here(d):
        for p in range(len(PARTS[d])):
            part(rb[d], d, p, 19).wait_recv()

    def absorb(d, right_ref, first):
        slot = jnp.int32(0)
        grade = jnp.float32(0.0)
        for r in range(SLOTS):
            hit = offs[r] == d
            slot = jnp.where(hit, r, slot)
            grade = jnp.where(hit, power_of_two(exps[r]), grade)
        left = own[slot]

        def one(s, carry):
            wanted = smeta[0, 0, s] - d
            t = jnp.int32(0)
            scale = jnp.float32(0.0)
            for j in range(NEED[d]):
                hit = smeta[d, 0, j] == wanted
                t = jnp.where(hit, j, t)
                scale = jnp.where(hit, power_of_two(smeta[d, 0, 8 + j]), scale)
            product = jnp.dot(left, right_ref[t], preferred_element_type=F32) * (grade * scale)
            if first:
                paths[s] = product
            else:
                paths[s] = paths[s] + product
            return carry

        lax.fori_loop(0 if d == 0 else max(1, d - 2), SLOTS, one, 0, unroll=True)

    for j in range(6):
        when(comes_down(j), has_come, own_down[j])
        if j == 0:
            when(c == 0, go, far_tile)
        when(even, go, on_facing[j])
        if j in ACROSS:
            when(both(odd, up_to(j, THIRD)), go, across[j])
        own_facing[j].wait_recv()
        if j < 3:
            when(both(odd, up_to(j, THIRD)) if j in ACROSS else up_to(j, THIRD), go, on_down[j])
        if j == 2:
            by_core(hand_on(1, 0), go)
            by_core(hand_on(2, 0), go)
            for copy in note_out:
                copy.wait_recv()
            to_scalar = pltpu.make_async_copy(meta, smeta, smeta_sem)
            to_scalar.start()
            to_scalar.wait()
            load_own.wait()
            absorb(0, own, True)
        if j == 3:
            v_on_down.start()
            when(c == 0, go, v_far)
            v_facing.start()
            v_down.start()
        if j == 4:
            by_core(hand_on(1, 1), go)
            by_core(hand_on(2, 1), go)
    by_core(hand_on(1, 2), go)
    absorb(4, rb4, False)
    absorb(2, rb2, False)
    for j in range(3):
        when(up_to(j, THIRD), has_come, on_down[j])
    by_core(hand_on(3, 0), go)
    absorb(6, rb6, False)
    for d in (1, 3, 5, 7):
        here(d)
        absorb(d, rb[d], False)


    ones = jnp.ones((8, TILE), BF16)
    degree = jnp.zeros((8, TILE), F32)
    for s in range(SLOTS):
        tile = ((own[s].astype(F32) * power_of_two(exps[s])) * paths[s]).astype(BF16)
        motif[s] = tile
        degree = degree + lax.dot_general(ones, tile, NT, preferred_element_type=F32)
    degree = degree[0:1, :]
    root = lax.rsqrt(degree)

    def exchange(xs, ssem, rsem):
        direct = [
            remote(xs.at[0], xs.at[2 * k], ssem.at[k], rsem.at[2 * k], at_blk(q - k, c)) for k in (1, 2, 3)
        ]
        far = remote(xs.at[0], xs.at[7], ssem.at[4], rsem.at[7], cross)
        near = remote(xs.at[0], xs.at[1], ssem.at[5], rsem.at[1], sibling)
        direct[2].start()
        by_core([far, near], go)
        direct[1].start()
        direct[0].start()
        return direct

    def passing(xs, ssem, rsem, k):
        return [
            remote(xs.at[2 * k], xs.at[d], ssem.at[5 + k], rsem.at[d], sibling)
            for d in (2 * k - 1, 2 * k + 1)
        ]

    def relay(xs, ssem, rsem, direct):
        for k in (1, 2, 3):
            direct[k - 1].wait_recv()
            by_core(passing(xs, ssem, rsem, k), go)

    def rest(xs, ssem, rsem):
        for d in (1, 3, 5, 7):
            remote(xs.at[d], xs.at[d], ssem.at[0], rsem.at[d], sibling).wait_recv()

    def all_left(xs, ssem, rsem, direct):
        for copy in direct:
            copy.wait_send()
        far = remote(xs.at[0], xs.at[7], ssem.at[4], rsem.at[7], cross)
        near = remote(xs.at[0], xs.at[1], ssem.at[5], rsem.at[1], sibling)
        by_core([far, near], left_here)
        for k in (1, 2, 3):
            by_core(passing(xs, ssem, rsem, k), left_here)

    def apply_graph(xs):
        total = jnp.zeros((VEC, TILE), F32)
        for s in range(SLOTS):
            total = total + lax.dot_general(xs[offs[s]], motif[s], NT, preferred_element_type=F32)
        return total

    lane = lax.broadcasted_iota(jnp.int32, (64, 128), 1)
    row = lax.broadcasted_iota(jnp.int32, (64, 128), 0)
    left = lane < VEC
    zeros = jnp.zeros((64, 128), F32)

    def gram(i, vectors):
        both = dot32(vectors, jnp.concatenate([vectors, vectors], axis=0), NT)
        g_src[i] = jnp.where(left[:32], both[:32], both[32:]) / NODES

    def copies_b(i):
        own_half, other_half = pl.ds(c * HALF, HALF), pl.ds((1 - c) * HALF, HALF)
        copies = []
        for j in range(NX):
            copies.append(remote(g_src.at[i, other_half], gb.at[i, j], gbs.at[i, j], gbr.at[i, j], x_others[j]))
            if j < NX - 1:
                n = NX + j
                copies.append(remote(g_src.at[i, own_half], gb.at[i, n], gbs.at[i, n], gbr.at[i, n], x_mates[j]))
        return copies

    def copies_c(i):
        return [remote(gc_src.at[i], gc.at[i, j], gcs.at[i, j], gcr.at[i, j], y_mates[j]) for j in range(NY - 1)]

    def copies_d(i):
        return [remote(gd_src.at[i], gd.at[i, j], gds.at[i, j], gdr.at[i, j], z_mates[j]) for j in range(NZ - 1)]

    def copies_e(i):
        mine = pl.ds(c * HALF, HALF)
        return [remote(fin.at[i, mine], fin.at[i, mine], ges.at[i], ger.at[i], sibling)]

    def start(copies):
        for copy in copies:
            copy.start()

    def arrive(copies):
        for copy in copies:
            copy.wait_recv()

    def step_b(i):
        start(copies_b(i))

    def step_c(i):
        arrive(copies_b(i))
        gc_src[i] = g_src[i, pl.ds(c * HALF, HALF), :] + sum(gb[i, j] for j in range(1, 7)) + gb[i, 0]
        start(copies_c(i))

    def step_d(i):
        arrive(copies_c(i))
        gd_src[i] = gc_src[i] + sum(gc[i, j] for j in range(1, 7)) + gc[i, 0]
        start(copies_d(i))

    def step_e(i):
        arrive(copies_d(i))
        fin[i, pl.ds(c * HALF, HALF), :] = gd_src[i] + sum(gd[i, j] for j in range(1, 7)) + gd[i, 0]
        start(copies_e(i))

    def collect(i):
        other = pl.ds((1 - c) * HALF, HALF)
        remote(fin.at[i, other], fin.at[i, other], ges.at[i], ger.at[i], sibling).wait_recv()
        packed = fin[i]
        turned = pltpu.roll(packed, 64, 1)
        return jnp.concatenate(
            [jnp.where(left[:32], packed, turned), jnp.where(left[:32], turned, packed)], axis=0
        )

    def left_all(copies):
        for copy in copies:
            copy.wait_send()

    def tiles_have_left():
        left_all(note_out + [v_down, v_facing, v_on_down])
        for j in range(SLOTS):
            when(comes_down(j), left_here, own_down[j])
            own_facing[j].wait_send()
            if j < 3:
                when(both(odd, up_to(j, THIRD)) if j in ACROSS else up_to(j, THIRD), left_here, on_down[j])
            if j in ACROSS:
                when(both(odd, up_to(j, THIRD)), left_here, across[j])

        @pl.when(c == 0)
        def _():
            left_all([far_tile, v_far])

        @pl.when(c == 1)
        def _():
            left_all(near_tiles + [v_near])

        for core in range(2):
            @pl.when(c == core)
            def _(core=core):
                for k in (1, 2, 3):
                    for p in range(3):
                        copy = hand_on(k, p)[core]
                        if copy is not None:
                            copy.wait_send()
                    v_hand_on[k][core].wait_send()

    roots[0] = root
    root_out = [
        remote(roots.at[0], roots.at[d], rsend.at[d], rrecv.at[d], at_behind(d)) for d in (7, 6, 5, 4, 3, 2, 1)
    ]
    start(root_out)
    v_facing.wait_recv()
    by_core(v_hand_on[1], go)
    v_down.wait_recv()
    by_core(v_hand_on[2], go)
    v_on_down.wait_recv()
    by_core(v_hand_on[3], go)
    tiles_have_left()
    for d in (1, 3, 5, 7):
        vectors(0, d, 0, sibling).wait_recv()
    arrive(root_out)
    total = jnp.zeros((VEC, TILE), F32)
    for s in range(SLOTS):
        input_s = (vs[offs[s]].astype(F32) * roots[offs[s]]).astype(BF16)
        total = total + lax.dot_general(input_s, motif[s], NT, preferred_element_type=F32)
    input_1 = (vs[0].astype(F32) * root).astype(BF16).astype(F32)
    scaled_1 = (total + degree * input_1) * root

    wide_2 = scaled_1 * root
    xs2[0] = wide_2.astype(BF16)
    sent_2 = exchange(xs2, x2s, x2r)
    gram(0, scaled_1)
    step_b(0)
    relay(xs2, x2s, x2r, sent_2)
    step_c(0)
    rest(xs2, x2s, x2r)
    scaled_2 = (apply_graph(xs2) + degree * wide_2) * root
    gram(1, scaled_2)
    step_b(1)
    step_d(0)
    step_c(1)
    left_all(root_out)
    all_left(xs2, x2s, x2r, sent_2)
    left_all(copies_b(0) + copies_c(0))
    step_e(0)
    step_d(1)
    gram_1 = collect(0)
    augmented = jnp.where(left, gram_1, jnp.where(lane == row + VEC, 1.0, 0.0))
    blocks = eliminate([augmented[8 * i : 8 * i + 8] for i in range(8)], 0, VEC)
    inverse_1 = jnp.where(left, 0.0, finish(blocks))
    left_all(copies_d(0) + copies_e(0) + copies_b(1) + copies_c(1))
    step_e(1)
    left_all(copies_d(1))
    gram_2 = jnp.where(left, 0.0, collect(1))
    half_way = dot32(inverse_1, jnp.concatenate([zeros, gram_2], axis=0))
    middle = dot32(half_way, jnp.concatenate([inverse_1, zeros], axis=0), NT)
    augmented = jnp.where(left, middle, inverse_1)
    blocks = eliminate([augmented[8 * i : 8 * i + 8] for i in range(8)], 0, VEC)
    inverse_2 = jnp.where(left, 0.0, finish(blocks))
    out[...] = dot32(inverse_2, jnp.concatenate([jnp.zeros((VEC, TILE), F32), scaled_2], axis=0))
    left_all(copies_e(1))


def shards(tile_values, tile_offset, tile_exponent, initial_vectors):
    dma = pltpu.SemaphoreType.DMA
    tiles = [pltpu.VMEM((ROWS[d], TILE, TILE), BF16) for d in range(1, REACH)]
    basis_t = pl.pallas_call(
        kernel,
        out_shape=jax.ShapeDtypeStruct((VEC, TILE), F32),
        in_specs=[
            pl.BlockSpec(memory_space=pltpu.HBM),
            pl.BlockSpec(memory_space=pltpu.HBM),
            pl.BlockSpec(memory_space=pltpu.HBM),
            pl.BlockSpec(memory_space=pltpu.HBM),
        ],
        out_specs=pl.BlockSpec(memory_space=pltpu.VMEM),
        scratch_shapes=[
            pltpu.VMEM((SLOTS, TILE, TILE), BF16),
            *tiles,
            pltpu.SMEM((1, SLOTS), jnp.int32),
            pltpu.SMEM((1, SLOTS), jnp.int32),
            pltpu.VMEM((REACH, 8, 128), jnp.int32),
            pltpu.SMEM((REACH, 8, 128), jnp.int32),
            pltpu.VMEM((SLOTS, TILE, TILE), F32),
            pltpu.VMEM((SLOTS, TILE, TILE), BF16),
            pltpu.VMEM((REACH, VEC, TILE), BF16),
            pltpu.VMEM((REACH, 1, TILE), F32),
            pltpu.VMEM((REACH, VEC, TILE), BF16),
            pltpu.VMEM((2, 2 * HALF, 128), F32),
            pltpu.VMEM((2, 2 * NX - 1, HALF, 128), F32),
            pltpu.VMEM((2, HALF, 128), F32),
            pltpu.VMEM((2, NY - 1, HALF, 128), F32),
            pltpu.VMEM((2, HALF, 128), F32),
            pltpu.VMEM((2, NZ - 1, HALF, 128), F32),
            pltpu.VMEM((2, 2 * HALF, 128), F32),
            dma, dma((3,)), dma,
            dma((31,)), dma((8, 6)), dma((8, 3)),
            dma((8,)), dma((8,)),
            dma((9,)), dma((8,)),
            dma((8,)), dma((8,)),
            dma((9,)), dma((8,)),
            dma((2, 2 * NX - 1)), dma((2, 2 * NX - 1)),
            dma((2, NY - 1)), dma((2, NY - 1)),
            dma((2, NZ - 1)), dma((2, NZ - 1)),
            dma((2,)), dma((2,)),
        ],
        compiler_params=pltpu.CompilerParams(
            collective_id=0, has_side_effects=True, vmem_limit_bytes=55000 * 1024
        ),
        cost_estimate=pl.CostEstimate(flops=1200000000, bytes_accessed=1000000, transcendentals=0),
        name="embed",
    )(tile_values, tile_offset, tile_exponent, initial_vectors.T)
    return basis_t.T


def solution(mesh):
    return jax.shard_map(
        shards,
        mesh=mesh,
        in_specs=(
            P(("grp", "blk"), None, None, None),
            P(("grp", "blk"), None),
            P(("grp", "blk"), None),
            P(("grp", "blk"), None),
        ),
        out_specs=P(("grp", "blk"), None),
        check_vma=False,
    )
```

```python
import jax
import jax.numpy as jnp
from jax import lax
from jax.experimental import pallas as pl
from jax.experimental.pallas import tpu as pltpu
from jax.sharding import PartitionSpec as P

TILE = 256
VEC = 64
SLOTS = 6
REACH = 8
NODES = 131072
BLK = 32
CHIPS = 16
NX, NY, NZ = 4, 8, 8
RING = (4, 3, 5, 2, 6, 1, 7)
HALF = 16
F32 = jnp.float32
BF16 = jnp.bfloat16
NEED = [min(SLOTS, REACH - d) for d in range(REACH)]
SECOND = [5, 4]
THIRD = [3, 2]
ACROSS = (1, 2)
PARTS = {1: [(0, 3), (3, 5), (5, 6)], 3: [(0, 3), (3, 5)], 5: [(0, 3)], 7: [(0, 1)]}
ROWS = {1: 6, 2: 6, 3: 5, 4: 6, 5: 3, 6: 3, 7: 1}
NT = (((1,), (1,)), ((), ()))


def power_of_two(e):
    one = jnp.float32(1.0)
    return jnp.where(
        e == -2, 0.25 * one,
        jnp.where(e == -1, 0.5 * one, jnp.where(e == 0, one, jnp.where(e == 1, 2 * one, 4 * one))),
    )


def dot32(a, b, dims=(((1,), (0,)), ((), ()))):
    return lax.dot_general(
        a, b, dims, precision=lax.Precision.HIGHEST, preferred_element_type=F32
    )


def reciprocal(x):
    guess = pl.reciprocal(x, approx=True)
    guess = guess * (2.0 - x * guess)
    return guess * (2.0 - x * guess)


def eliminate(blocks, first, last):
    blocks = list(blocks)
    sub = lax.broadcasted_iota(jnp.int32, (8, 128), 0)

    def spread(row):
        return jnp.broadcast_to(row, (8, 128))

    for k in range(first, last, 4):
        kb, kr = divmod(k, 8)
        head = blocks[kb]
        columns = {
            i: [spread(blocks[i][:, k + j : k + j + 1]) for j in range(4)]
            for i in range(kb, 8)
        }
        upper = [spread(head[kr + j : kr + j + 1, :]) for j in range(4)]
        corner = [[spread(columns[kb][j][kr + a : kr + a + 1, :]) for j in range(4)] for a in range(4)]
        inverse = []
        for a in (0, 2):
            inverse.append(reciprocal(corner[a][a]))
            low = corner[a][a + 1] * inverse[a]
            minor = corner[a][a] * corner[a + 1][a + 1] - corner[a][a + 1] * corner[a][a + 1]
            inverse.append(corner[a][a] * reciprocal(minor))
            for j in range(a + 1, 4):
                corner[a + 1][j] = corner[a + 1][j] - low * corner[a][j]
            upper[a + 1] = upper[a + 1] - low * upper[a]
            for r in range(a + 2, 4):
                for e in (a, a + 1):
                    low = corner[e][r] * inverse[e]
                    for j in range(r, 4):
                        corner[r][j] = corner[r][j] - low * corner[e][j]
                    upper[r] = upper[r] - low * upper[e]
        for i in range(kb, 8):
            if i == kb and kr == 4:
                continue
            block = blocks[i]
            factors = []
            for a in range(4):
                rest = columns[i][a]
                for e in range(a):
                    rest = rest - factors[e] * corner[e][a]
                factors.append(rest * inverse[a])
            for a in range(4):
                block = block - factors[a] * upper[a]
            blocks[i] = block if i > kb else jnp.where(sub > kr + 3, block, head)
        done = blocks[kb]
        for a in range(4):
            done = jnp.where(sub == kr + a, upper[a], done)
        blocks[kb] = done
    return blocks


def finish(blocks):
    lane = lax.broadcasted_iota(jnp.int32, (8, 128), 1)
    sub = lax.broadcasted_iota(jnp.int32, (8, 128), 0)
    done = []
    for i, block in enumerate(blocks):
        pivot = jnp.sum(jnp.where(lane == sub + 8 * i, block, 0.0), axis=1, keepdims=True)
        done.append(block * lax.rsqrt(pivot))
    return jnp.concatenate(done, axis=0)


def kernel(
    tv, off_any, ex_any, v0, out,
    own, rb1, rb2, rb3, rb4, rb5, rb6, rb7, off, ex, meta, smeta, paths, motif, vs, roots, xs2,
    g_src, gb, gc_src, gc, gd_src, gd, fin,
    own_sem, in_sem, smeta_sem, ts, tr, tp, ms, mr, vsend, vrecv, rsend, rrecv, x2s, x2r,
    gbs, gbr, gcs, gcr, gds, gdr, ges, ger,
):
    rb = {1: rb1, 2: rb2, 3: rb3, 4: rb4, 5: rb5, 6: rb6, 7: rb7}
    g = lax.axis_index("grp")
    b = lax.axis_index("blk")
    c = lax.rem(b, 2)
    q = b // 2
    x_hi, z = lax.rem(q, 2), q // 2
    x_lo, y = lax.rem(g, 2), g // 2
    x = x_hi * 2 + x_lo

    def at_blk(chip, core):
        return {"grp": g, "blk": lax.rem(chip + 2 * CHIPS, CHIPS) * 2 + core}

    def at_behind(d):
        return {"grp": g, "blk": lax.rem(b + BLK - d, BLK)}

    def at_xyz(xx, yy, zz, core=c):
        return {
            "grp": yy * 2 + lax.rem(xx, 2),
            "blk": (zz * 2 + xx // 2) * 2 + core,
        }

    sibling = at_blk(q, 1 - c)
    cross = at_blk(q - 4 + 8 * c, 1 - c)
    facing = at_blk(q + 1 - 2 * x_hi, c)
    even, odd = x_hi == 0, x_hi == 1
    below = at_blk(q - 2, c)
    x_mates = [at_xyz(lax.rem(x + j, NX), y, z) for j in (2, 1, 3)]
    x_others = [at_xyz(lax.rem(x + j, NX), y, z, 1 - c) for j in (2, 1, 3, 0)]
    y_mates = [at_xyz(x, lax.rem(y + j, NY), z) for j in RING]
    z_mates = [at_xyz(x, y, lax.rem(z + j, NZ)) for j in RING]

    def remote(src, dst, ssem, rsem, dev):
        return pltpu.make_async_remote_copy(
            src_ref=src, dst_ref=dst, send_sem=ssem, recv_sem=rsem,
            device_id=dev, device_id_type=pl.DeviceIdType.MESH,
        )

    barrier = pltpu.get_barrier_semaphore()
    met = y_mates + z_mates[:5] + x_mates[1:] + x_others[1:3]
    for d in range(REACH - 1, 0, -1):
        met.append(at_behind(d))
        met.append(at_behind(-d))
    for dev in met:
        pl.semaphore_signal(barrier, inc=1, device_id=dev, device_id_type=pl.DeviceIdType.MESH)

    load_own = pltpu.make_async_copy(tv.at[0], own, own_sem)
    load_own.start()
    load_off = pltpu.make_async_copy(off_any, off, in_sem.at[0])
    load_ex = pltpu.make_async_copy(ex_any, ex, in_sem.at[1])
    load_off.start()
    load_ex.start()
    load_v0 = pltpu.make_async_copy(v0, vs.at[0], in_sem.at[2])
    load_v0.start()

    load_off.wait()
    load_ex.wait()
    offs = [off[0, s] for s in range(SLOTS)]
    exps = [ex[0, s] for s in range(SLOTS)]
    lane8 = lax.broadcasted_iota(jnp.int32, (8, 128), 1)
    note = jnp.zeros((8, 128), jnp.int32)
    for s in range(SLOTS):
        note = jnp.where(lane8 == s, offs[s], note)
        note = jnp.where(lane8 == 8 + s, exps[s], note)
    meta[0] = note
    pl.semaphore_wait(barrier, len(met))

    def one_tile(src, d, j, sem, dev):
        return remote(src.at[j], rb[d].at[j], ts.at[sem + j], tr.at[d, j], dev)

    mine = tv.at[0]
    own_down = [one_tile(mine, 4, j, 0, below) for j in range(6)]
    own_facing = [one_tile(mine, 2, j, 6, facing) for j in range(6)]
    on_facing = [one_tile(rb4, 2, j, 6, facing) for j in range(6)]
    on_down = [one_tile(rb2, 6, j, 12, below) for j in range(3)]
    across = [one_tile(rb4, 6, j, 15, facing) for j in range(3)]
    far_tile = remote(rb4.at[0], rb7.at[0], ts.at[18], tp.at[7, 0], at_blk(q - 2, 1))

    def both(*tests):
        keep = tests[0]
        for test in tests[1:]:
            keep = jnp.logical_and(keep, test)
        return keep

    def up_to(j, limits):
        return c >= 0 if j < limits[1] else (c == 0 if j < limits[0] else c < 0)

    def comes_down(j):
        return jnp.logical_or(even, up_to(j, SECOND))

    def part(src, d, p, sem):
        lo, hi = PARTS[d][p]
        return remote(src.at[pl.ds(lo, hi - lo)], rb[d].at[pl.ds(lo, hi - lo)], ts.at[sem + p], tp.at[d, p], sibling)

    def vectors(src, d, sem, dev):
        return remote(vs.at[src], vs.at[d], vsend.at[sem], vrecv.at[d], dev)

    v_down = vectors(0, 4, 0, below)
    v_facing = vectors(0, 2, 1, at_blk(q - 1, c))
    v_on_down = vectors(0, 6, 2, at_blk(q - 3, c))
    v_far = vectors(0, 7, 4, cross)
    v_near = vectors(0, 1, 5, sibling)
    v_hand_on = [None] + [[vectors(2 * k, d, 5 + k, sibling) for d in (2 * k - 1, 2 * k + 1)] for k in (1, 2, 3)]

    near_tiles = [part(mine, 1, p, 19) for p in range(3)]
    note_out = [
        remote(meta.at[0], meta.at[d], ms.at[d], mr.at[d], at_behind(d)) for d in range(REACH - 1, 0, -1)
    ]
    def by_core(copies, act):
        for core in range(2):
            if copies[core] is not None:
                @pl.when(c == core)
                def _(copy=copies[core]):
                    act(copy)

    def go(copy):
        copy.start()

    def left_here(copy):
        copy.wait_send()

    def has_come(copy):
        copy.wait_recv()

    def when(test, act, copy):
        @pl.when(test)
        def _():
            act(copy)

    for copy in note_out:
        copy.start()
    for j in range(SLOTS):
        when(odd, go, own_facing[j])
        when(comes_down(j), go, own_down[j])
    load_v0.wait()
    when(c == 1, go, v_near)

    @pl.when(c == 1)
    def _():
        for copy in near_tiles:
            copy.start()

    def hand_on(k, p):
        return [
            part(rb[2 * k], d, p, 19 + 3 * k) if p < len(PARTS[d]) else None
            for d in (2 * k - 1, 2 * k + 1)
        ]

    def here(d):
        for p in range(len(PARTS[d])):
            part(rb[d], d, p, 19).wait_recv()

    def absorb(d, right_ref, first):
        slot = jnp.int32(0)
        grade = jnp.float32(0.0)
        for r in range(SLOTS):
            hit = offs[r] == d
            slot = jnp.where(hit, r, slot)
            grade = jnp.where(hit, power_of_two(exps[r]), grade)
        left = own[slot]

        def one(s, carry):
            wanted = smeta[0, 0, s] - d
            t = jnp.int32(0)
            scale = jnp.float32(0.0)
            for j in range(NEED[d]):
                hit = smeta[d, 0, j] == wanted
                t = jnp.where(hit, j, t)
                scale = jnp.where(hit, power_of_two(smeta[d, 0, 8 + j]), scale)
            product = jnp.dot(left, right_ref[t], preferred_element_type=F32) * (grade * scale)
            if first:
                paths[s] = product
            else:
                paths[s] = paths[s] + product
            return carry

        lax.fori_loop(0 if d == 0 else max(1, d - 2), SLOTS, one, 0, unroll=True)

    for j in range(6):
        when(comes_down(j), has_come, own_down[j])
        if j == 0:
            when(c == 0, go, far_tile)
        when(even, go, on_facing[j])
        if j in ACROSS:
            when(both(odd, up_to(j, THIRD)), go, across[j])
        own_facing[j].wait_recv()
        if j < 3:
            when(both(odd, up_to(j, THIRD)) if j in ACROSS else up_to(j, THIRD), go, on_down[j])
        if j == 2:
            by_core(hand_on(1, 0), go)
            by_core(hand_on(2, 0), go)
            for copy in note_out:
                copy.wait_recv()
            to_scalar = pltpu.make_async_copy(meta, smeta, smeta_sem)
            to_scalar.start()
            to_scalar.wait()
            load_own.wait()
            absorb(0, own, True)
        if j == 3:
            v_on_down.start()
            when(c == 0, go, v_far)
            v_facing.start()
            v_down.start()
        if j == 4:
            by_core(hand_on(1, 1), go)
            by_core(hand_on(2, 1), go)
    by_core(hand_on(1, 2), go)
    absorb(4, rb4, False)
    absorb(2, rb2, False)
    for j in range(3):
        when(up_to(j, THIRD), has_come, on_down[j])
    by_core(hand_on(3, 0), go)
    absorb(6, rb6, False)
    for d in (1, 3, 5, 7):
        here(d)
        absorb(d, rb[d], False)


    ones = jnp.ones((8, TILE), BF16)
    degree = jnp.zeros((8, TILE), F32)
    for s in range(SLOTS):
        tile = ((own[s].astype(F32) * power_of_two(exps[s])) * paths[s]).astype(BF16)
        motif[s] = tile
        degree = degree + lax.dot_general(ones, tile, NT, preferred_element_type=F32)
    degree = degree[0:1, :]
    root = lax.rsqrt(degree)

    def exchange(xs, ssem, rsem):
        direct = [
            remote(xs.at[0], xs.at[2 * k], ssem.at[k], rsem.at[2 * k], at_blk(q - k, c)) for k in (1, 2, 3)
        ]
        far = remote(xs.at[0], xs.at[7], ssem.at[4], rsem.at[7], cross)
        near = remote(xs.at[0], xs.at[1], ssem.at[5], rsem.at[1], sibling)
        direct[2].start()
        direct[1].start()
        direct[0].start()
        by_core([far, near], go)
        return direct

    def passing(xs, ssem, rsem, k):
        return [
            remote(xs.at[2 * k], xs.at[d], ssem.at[5 + k], rsem.at[d], sibling)
            for d in (2 * k - 1, 2 * k + 1)
        ]

    def relay(xs, ssem, rsem, direct):
        for k in (1, 2, 3):
            direct[k - 1].wait_recv()
            by_core(passing(xs, ssem, rsem, k), go)

    def rest(xs, ssem, rsem):
        for d in (1, 3, 5, 7):
            remote(xs.at[d], xs.at[d], ssem.at[0], rsem.at[d], sibling).wait_recv()

    def all_left(xs, ssem, rsem, direct):
        for copy in direct:
            copy.wait_send()
        far = remote(xs.at[0], xs.at[7], ssem.at[4], rsem.at[7], cross)
        near = remote(xs.at[0], xs.at[1], ssem.at[5], rsem.at[1], sibling)
        by_core([far, near], left_here)
        for k in (1, 2, 3):
            by_core(passing(xs, ssem, rsem, k), left_here)

    def apply_graph(xs):
        total = jnp.zeros((VEC, TILE), F32)
        for s in range(SLOTS):
            total = total + lax.dot_general(xs[offs[s]], motif[s], NT, preferred_element_type=F32)
        return total

    lane = lax.broadcasted_iota(jnp.int32, (64, 128), 1)
    row = lax.broadcasted_iota(jnp.int32, (64, 128), 0)
    left = lane < VEC
    zeros = jnp.zeros((64, 128), F32)

    def gram(i, vectors):
        both = dot32(vectors, jnp.concatenate([vectors, vectors], axis=0), NT)
        g_src[i] = jnp.where(left[:32], both[:32], both[32:]) / NODES

    def copies_b(i):
        own_half, other_half = pl.ds(c * HALF, HALF), pl.ds((1 - c) * HALF, HALF)
        copies = []
        for j in range(NX):
            copies.append(remote(g_src.at[i, other_half], gb.at[i, j], gbs.at[i, j], gbr.at[i, j], x_others[j]))
            if j < NX - 1:
                n = NX + j
                copies.append(remote(g_src.at[i, own_half], gb.at[i, n], gbs.at[i, n], gbr.at[i, n], x_mates[j]))
        return copies

    def copies_c(i):
        return [remote(gc_src.at[i], gc.at[i, j], gcs.at[i, j], gcr.at[i, j], y_mates[j]) for j in range(NY - 1)]

    def copies_d(i):
        return [remote(gd_src.at[i], gd.at[i, j], gds.at[i, j], gdr.at[i, j], z_mates[j]) for j in range(NZ - 1)]

    def copies_e(i):
        mine = pl.ds(c * HALF, HALF)
        return [remote(fin.at[i, mine], fin.at[i, mine], ges.at[i], ger.at[i], sibling)]

    def start(copies):
        for copy in copies:
            copy.start()

    def arrive(copies):
        for copy in copies:
            copy.wait_recv()

    def step_b(i):
        start(copies_b(i))

    def step_c(i):
        arrive(copies_b(i))
        gc_src[i] = g_src[i, pl.ds(c * HALF, HALF), :] + sum(gb[i, j] for j in range(1, 7)) + gb[i, 0]
        start(copies_c(i))

    def step_d(i):
        arrive(copies_c(i))
        gd_src[i] = gc_src[i] + sum(gc[i, j] for j in range(1, 7)) + gc[i, 0]
        start(copies_d(i))

    def step_e(i):
        arrive(copies_d(i))
        fin[i, pl.ds(c * HALF, HALF), :] = gd_src[i] + sum(gd[i, j] for j in range(1, 7)) + gd[i, 0]
        start(copies_e(i))

    def collect(i):
        other = pl.ds((1 - c) * HALF, HALF)
        remote(fin.at[i, other], fin.at[i, other], ges.at[i], ger.at[i], sibling).wait_recv()
        packed = fin[i]
        turned = pltpu.roll(packed, 64, 1)
        return jnp.concatenate(
            [jnp.where(left[:32], packed, turned), jnp.where(left[:32], turned, packed)], axis=0
        )

    def left_all(copies):
        for copy in copies:
            copy.wait_send()

    def tiles_have_left():
        left_all(note_out + [v_down, v_facing, v_on_down])
        for j in range(SLOTS):
            when(comes_down(j), left_here, own_down[j])
            own_facing[j].wait_send()
            if j < 3:
                when(both(odd, up_to(j, THIRD)) if j in ACROSS else up_to(j, THIRD), left_here, on_down[j])
            if j in ACROSS:
                when(both(odd, up_to(j, THIRD)), left_here, across[j])

        @pl.when(c == 0)
        def _():
            left_all([far_tile, v_far])

        @pl.when(c == 1)
        def _():
            left_all(near_tiles + [v_near])

        for core in range(2):
            @pl.when(c == core)
            def _(core=core):
                for k in (1, 2, 3):
                    for p in range(3):
                        copy = hand_on(k, p)[core]
                        if copy is not None:
                            copy.wait_send()
                    v_hand_on[k][core].wait_send()

    roots[0] = root
    root_out = [
        remote(roots.at[0], roots.at[d], rsend.at[d], rrecv.at[d], at_behind(d)) for d in (7, 6, 5, 4, 3, 2, 1)
    ]
    start(root_out)
    v_facing.wait_recv()
    by_core(v_hand_on[1], go)
    v_down.wait_recv()
    by_core(v_hand_on[2], go)
    v_on_down.wait_recv()
    by_core(v_hand_on[3], go)
    tiles_have_left()
    for d in (1, 3, 5, 7):
        vectors(0, d, 0, sibling).wait_recv()
    arrive(root_out)
    total = jnp.zeros((VEC, TILE), F32)
    for s in range(SLOTS):
        input_s = (vs[offs[s]].astype(F32) * roots[offs[s]]).astype(BF16)
        total = total + lax.dot_general(input_s, motif[s], NT, preferred_element_type=F32)
    input_1 = (vs[0].astype(F32) * root).astype(BF16).astype(F32)
    scaled_1 = (total + degree * input_1) * root

    wide_2 = scaled_1 * root
    xs2[0] = wide_2.astype(BF16)
    sent_2 = exchange(xs2, x2s, x2r)
    gram(0, scaled_1)
    step_b(0)
    relay(xs2, x2s, x2r, sent_2)
    step_c(0)
    rest(xs2, x2s, x2r)
    scaled_2 = (apply_graph(xs2) + degree * wide_2) * root
    gram(1, scaled_2)
    step_b(1)
    step_d(0)
    step_c(1)
    left_all(root_out)
    all_left(xs2, x2s, x2r, sent_2)
    left_all(copies_b(0) + copies_c(0))
    step_e(0)
    step_d(1)
    gram_1 = collect(0)
    augmented = jnp.where(left, gram_1, jnp.where(lane == row + VEC, 1.0, 0.0))
    blocks = eliminate([augmented[8 * i : 8 * i + 8] for i in range(8)], 0, VEC)
    inverse_1 = jnp.where(left, 0.0, finish(blocks))
    left_all(copies_d(0) + copies_e(0) + copies_b(1) + copies_c(1))
    step_e(1)
    left_all(copies_d(1))
    gram_2 = jnp.where(left, 0.0, collect(1))
    half_way = dot32(inverse_1, jnp.concatenate([zeros, gram_2], axis=0))
    middle = dot32(half_way, jnp.concatenate([inverse_1, zeros], axis=0), NT)
    augmented = jnp.where(left, middle, inverse_1)
    blocks = eliminate([augmented[8 * i : 8 * i + 8] for i in range(8)], 0, VEC)
    inverse_2 = jnp.where(left, 0.0, finish(blocks))
    out[...] = dot32(inverse_2, jnp.concatenate([jnp.zeros((VEC, TILE), F32), scaled_2], axis=0))
    left_all(copies_e(1))


def shards(tile_values, tile_offset, tile_exponent, initial_vectors):
    dma = pltpu.SemaphoreType.DMA
    tiles = [pltpu.VMEM((ROWS[d], TILE, TILE), BF16) for d in range(1, REACH)]
    basis_t = pl.pallas_call(
        kernel,
        out_shape=jax.ShapeDtypeStruct((VEC, TILE), F32),
        in_specs=[
            pl.BlockSpec(memory_space=pltpu.HBM),
            pl.BlockSpec(memory_space=pltpu.HBM),
            pl.BlockSpec(memory_space=pltpu.HBM),
            pl.BlockSpec(memory_space=pltpu.HBM),
        ],
        out_specs=pl.BlockSpec(memory_space=pltpu.VMEM),
        scratch_shapes=[
            pltpu.VMEM((SLOTS, TILE, TILE), BF16),
            *tiles,
            pltpu.SMEM((1, SLOTS), jnp.int32),
            pltpu.SMEM((1, SLOTS), jnp.int32),
            pltpu.VMEM((REACH, 8, 128), jnp.int32),
            pltpu.SMEM((REACH, 8, 128), jnp.int32),
            pltpu.VMEM((SLOTS, TILE, TILE), F32),
            pltpu.VMEM((SLOTS, TILE, TILE), BF16),
            pltpu.VMEM((REACH, VEC, TILE), BF16),
            pltpu.VMEM((REACH, 1, TILE), F32),
            pltpu.VMEM((REACH, VEC, TILE), BF16),
            pltpu.VMEM((2, 2 * HALF, 128), F32),
            pltpu.VMEM((2, 2 * NX - 1, HALF, 128), F32),
            pltpu.VMEM((2, HALF, 128), F32),
            pltpu.VMEM((2, NY - 1, HALF, 128), F32),
            pltpu.VMEM((2, HALF, 128), F32),
            pltpu.VMEM((2, NZ - 1, HALF, 128), F32),
            pltpu.VMEM((2, 2 * HALF, 128), F32),
            dma, dma((3,)), dma,
            dma((31,)), dma((8, 6)), dma((8, 3)),
            dma((8,)), dma((8,)),
            dma((9,)), dma((8,)),
            dma((8,)), dma((8,)),
            dma((9,)), dma((8,)),
            dma((2, 2 * NX - 1)), dma((2, 2 * NX - 1)),
            dma((2, NY - 1)), dma((2, NY - 1)),
            dma((2, NZ - 1)), dma((2, NZ - 1)),
            dma((2,)), dma((2,)),
        ],
        compiler_params=pltpu.CompilerParams(
            collective_id=0, has_side_effects=True, vmem_limit_bytes=55000 * 1024
        ),
        cost_estimate=pl.CostEstimate(flops=1200000000, bytes_accessed=1000000, transcendentals=0),
        name="embed",
    )(tile_values, tile_offset, tile_exponent, initial_vectors.T)
    return basis_t.T


def solution(mesh):
    return jax.shard_map(
        shards,
        mesh=mesh,
        in_specs=(
            P(("grp", "blk"), None, None, None),
            P(("grp", "blk"), None),
            P(("grp", "blk"), None),
            P(("grp", "blk"), None),
        ),
        out_specs=P(("grp", "blk"), None),
        check_vma=False,
    )
```

```python
import jax
import jax.numpy as jnp
from jax import lax
from jax.experimental import pallas as pl
from jax.experimental.pallas import tpu as pltpu
from jax.sharding import PartitionSpec as P

TILE = 256
VEC = 64
SLOTS = 6
REACH = 8
NODES = 131072
BLK = 32
CHIPS = 16
NX, NY, NZ = 4, 8, 8
RING = (4, 3, 5, 2, 6, 1, 7)
HALF = 16
F32 = jnp.float32
BF16 = jnp.bfloat16
NEED = [min(SLOTS, REACH - d) for d in range(REACH)]
SECOND = [5, 4]
THIRD = [3, 2]
ACROSS = (1, 2)
PARTS = {1: [(0, 3), (3, 5), (5, 6)], 3: [(0, 3), (3, 5)], 5: [(0, 3)], 7: [(0, 1)]}
ROWS = {1: 6, 2: 6, 3: 5, 4: 6, 5: 3, 6: 3, 7: 1}
NT = (((1,), (1,)), ((), ()))


def power_of_two(e):
    one = jnp.float32(1.0)
    return jnp.where(
        e == -2, 0.25 * one,
        jnp.where(e == -1, 0.5 * one, jnp.where(e == 0, one, jnp.where(e == 1, 2 * one, 4 * one))),
    )


def dot32(a, b, dims=(((1,), (0,)), ((), ()))):
    return lax.dot_general(
        a, b, dims, precision=lax.Precision.HIGHEST, preferred_element_type=F32
    )


def reciprocal(x):
    guess = pl.reciprocal(x, approx=True)
    guess = guess * (2.0 - x * guess)
    return guess * (2.0 - x * guess)


def eliminate(blocks, first, last):
    blocks = list(blocks)
    sub = lax.broadcasted_iota(jnp.int32, (8, 128), 0)

    def spread(row):
        return jnp.broadcast_to(row, (8, 128))

    for k in range(first, last, 4):
        kb, kr = divmod(k, 8)
        head = blocks[kb]
        columns = {
            i: [spread(blocks[i][:, k + j : k + j + 1]) for j in range(4)]
            for i in range(kb, 8)
        }
        upper = [spread(head[kr + j : kr + j + 1, :]) for j in range(4)]
        corner = [[spread(columns[kb][j][kr + a : kr + a + 1, :]) for j in range(4)] for a in range(4)]
        inverse = []
        for a in (0, 2):
            inverse.append(reciprocal(corner[a][a]))
            low = corner[a][a + 1] * inverse[a]
            minor = corner[a][a] * corner[a + 1][a + 1] - corner[a][a + 1] * corner[a][a + 1]
            inverse.append(corner[a][a] * reciprocal(minor))
            for j in range(a + 1, 4):
                corner[a + 1][j] = corner[a + 1][j] - low * corner[a][j]
            upper[a + 1] = upper[a + 1] - low * upper[a]
            for r in range(a + 2, 4):
                for e in (a, a + 1):
                    low = corner[e][r] * inverse[e]
                    for j in range(r, 4):
                        corner[r][j] = corner[r][j] - low * corner[e][j]
                    upper[r] = upper[r] - low * upper[e]
        for i in range(kb, 8):
            if i == kb and kr == 4:
                continue
            block = blocks[i]
            factors = []
            for a in range(4):
                rest = columns[i][a]
                for e in range(a):
                    rest = rest - factors[e] * corner[e][a]
                factors.append(rest * inverse[a])
            for a in range(4):
                block = block - factors[a] * upper[a]
            blocks[i] = block if i > kb else jnp.where(sub > kr + 3, block, head)
        done = blocks[kb]
        for a in range(4):
            done = jnp.where(sub == kr + a, upper[a], done)
        blocks[kb] = done
    return blocks


def finish(blocks):
    lane = lax.broadcasted_iota(jnp.int32, (8, 128), 1)
    sub = lax.broadcasted_iota(jnp.int32, (8, 128), 0)
    done = []
    for i, block in enumerate(blocks):
        pivot = jnp.sum(jnp.where(lane == sub + 8 * i, block, 0.0), axis=1, keepdims=True)
        done.append(block * lax.rsqrt(pivot))
    return jnp.concatenate(done, axis=0)


def kernel(
    tv, off_any, ex_any, v0, out,
    own, rb1, rb2, rb3, rb4, rb5, rb6, rb7, off, ex, meta, smeta, paths, motif, vs, roots, xs2,
    g_src, gb, gc_src, gc, gd_src, gd, fin,
    own_sem, in_sem, smeta_sem, ts, tr, tp, ms, mr, vsend, vrecv, rsend, rrecv, x2s, x2r,
    gbs, gbr, gcs, gcr, gds, gdr, ges, ger,
):
    rb = {1: rb1, 2: rb2, 3: rb3, 4: rb4, 5: rb5, 6: rb6, 7: rb7}
    g = lax.axis_index("grp")
    b = lax.axis_index("blk")
    c = lax.rem(b, 2)
    q = b // 2
    x_hi, z = lax.rem(q, 2), q // 2
    x_lo, y = lax.rem(g, 2), g // 2
    x = x_hi * 2 + x_lo

    def at_blk(chip, core):
        return {"grp": g, "blk": lax.rem(chip + 2 * CHIPS, CHIPS) * 2 + core}

    def at_behind(d):
        return {"grp": g, "blk": lax.rem(b + BLK - d, BLK)}

    def at_xyz(xx, yy, zz, core=c):
        return {
            "grp": yy * 2 + lax.rem(xx, 2),
            "blk": (zz * 2 + xx // 2) * 2 + core,
        }

    sibling = at_blk(q, 1 - c)
    cross = at_blk(q - 4 + 8 * c, 1 - c)
    facing = at_blk(q + 1 - 2 * x_hi, c)
    even, odd = x_hi == 0, x_hi == 1
    below = at_blk(q - 2, c)
    x_mates = [at_xyz(lax.rem(x + j, NX), y, z) for j in (2, 1, 3)]
    x_others = [at_xyz(lax.rem(x + j, NX), y, z, 1 - c) for j in (2, 1, 3, 0)]
    y_mates = [at_xyz(x, lax.rem(y + j, NY), z) for j in RING]
    z_mates = [at_xyz(x, y, lax.rem(z + j, NZ)) for j in RING]

    def remote(src, dst, ssem, rsem, dev):
        return pltpu.make_async_remote_copy(
            src_ref=src, dst_ref=dst, send_sem=ssem, recv_sem=rsem,
            device_id=dev, device_id_type=pl.DeviceIdType.MESH,
        )

    barrier = pltpu.get_barrier_semaphore()
    met = y_mates + z_mates[:5] + x_mates[1:] + x_others[1:3]
    for d in range(REACH - 1, 0, -1):
        met.append(at_behind(d))
        met.append(at_behind(-d))
    for dev in met:
        pl.semaphore_signal(barrier, inc=1, device_id=dev, device_id_type=pl.DeviceIdType.MESH)

    load_own = pltpu.make_async_copy(tv.at[0], own, own_sem)
    load_own.start()
    load_off = pltpu.make_async_copy(off_any, off, in_sem.at[0])
    load_ex = pltpu.make_async_copy(ex_any, ex, in_sem.at[1])
    load_off.start()
    load_ex.start()
    load_v0 = pltpu.make_async_copy(v0, vs.at[0], in_sem.at[2])
    load_v0.start()

    load_off.wait()
    load_ex.wait()
    offs = [off[0, s] for s in range(SLOTS)]
    exps = [ex[0, s] for s in range(SLOTS)]
    lane8 = lax.broadcasted_iota(jnp.int32, (8, 128), 1)
    note = jnp.zeros((8, 128), jnp.int32)
    for s in range(SLOTS):
        note = jnp.where(lane8 == s, offs[s], note)
        note = jnp.where(lane8 == 8 + s, exps[s], note)
    meta[0] = note
    pl.semaphore_wait(barrier, len(met))

    def one_tile(src, d, j, sem, dev):
        return remote(src.at[j], rb[d].at[j], ts.at[sem + j], tr.at[d, j], dev)

    mine = tv.at[0]
    own_down = [one_tile(mine, 4, j, 0, below) for j in range(6)]
    own_facing = [one_tile(mine, 2, j, 6, facing) for j in range(6)]
    on_facing = [one_tile(rb4, 2, j, 6, facing) for j in range(6)]
    on_down = [one_tile(rb2, 6, j, 12, below) for j in range(3)]
    across = [one_tile(rb4, 6, j, 15, facing) for j in range(3)]
    far_tile = remote(rb4.at[0], rb7.at[0], ts.at[18], tp.at[7, 0], at_blk(q - 2, 1))

    def both(*tests):
        keep = tests[0]
        for test in tests[1:]:
            keep = jnp.logical_and(keep, test)
        return keep

    def up_to(j, limits):
        return c >= 0 if j < limits[1] else (c == 0 if j < limits[0] else c < 0)

    def comes_down(j):
        return jnp.logical_or(even, up_to(j, SECOND))

    def part(src, d, p, sem):
        lo, hi = PARTS[d][p]
        return remote(src.at[pl.ds(lo, hi - lo)], rb[d].at[pl.ds(lo, hi - lo)], ts.at[sem + p], tp.at[d, p], sibling)

    def vectors(src, d, sem, dev):
        return remote(vs.at[src], vs.at[d], vsend.at[sem], vrecv.at[d], dev)

    v_down = vectors(0, 4, 0, below)
    v_facing = vectors(0, 2, 1, at_blk(q - 1, c))
    v_on_down = vectors(0, 6, 2, at_blk(q - 3, c))
    v_far = vectors(0, 7, 4, cross)
    v_near = vectors(0, 1, 5, sibling)
    v_hand_on = [None] + [[vectors(2 * k, d, 5 + k, sibling) for d in (2 * k - 1, 2 * k + 1)] for k in (1, 2, 3)]

    near_tiles = [part(mine, 1, p, 19) for p in range(3)]
    note_out = [
        remote(meta.at[0], meta.at[d], ms.at[d], mr.at[d], at_behind(d)) for d in range(REACH - 1, 0, -1)
    ]
    def by_core(copies, act):
        for core in range(2):
            if copies[core] is not None:
                @pl.when(c == core)
                def _(copy=copies[core]):
                    act(copy)

    def go(copy):
        copy.start()

    def left_here(copy):
        copy.wait_send()

    def has_come(copy):
        copy.wait_recv()

    def when(test, act, copy):
        @pl.when(test)
        def _():
            act(copy)

    for copy in note_out:
        copy.start()
    for j in range(SLOTS):
        when(odd, go, own_facing[j])
        when(comes_down(j), go, own_down[j])
    load_v0.wait()
    when(c == 1, go, v_near)

    @pl.when(c == 1)
    def _():
        for copy in near_tiles:
            copy.start()

    def hand_on(k, p):
        return [
            part(rb[2 * k], d, p, 19 + 3 * k) if p < len(PARTS[d]) else None
            for d in (2 * k - 1, 2 * k + 1)
        ]

    def here(d):
        for p in range(len(PARTS[d])):
            part(rb[d], d, p, 19).wait_recv()

    def absorb(d, right_ref, first):
        slot = jnp.int32(0)
        grade = jnp.float32(0.0)
        for r in range(SLOTS):
            hit = offs[r] == d
            slot = jnp.where(hit, r, slot)
            grade = jnp.where(hit, power_of_two(exps[r]), grade)
        left = own[slot]

        def one(s, carry):
            wanted = smeta[0, 0, s] - d
            t = jnp.int32(0)
            scale = jnp.float32(0.0)
            for j in range(NEED[d]):
                hit = smeta[d, 0, j] == wanted
                t = jnp.where(hit, j, t)
                scale = jnp.where(hit, power_of_two(smeta[d, 0, 8 + j]), scale)
            product = jnp.dot(left, right_ref[t], preferred_element_type=F32) * (grade * scale)
            if first:
                paths[s] = product
            else:
                paths[s] = paths[s] + product
            return carry

        lax.fori_loop(0 if d == 0 else max(1, d - 2), SLOTS, one, 0, unroll=True)

    for j in range(6):
        when(comes_down(j), has_come, own_down[j])
        if j == 0:
            when(c == 0, go, far_tile)
        when(even, go, on_facing[j])
        if j in ACROSS:
            when(both(odd, up_to(j, THIRD)), go, across[j])
        own_facing[j].wait_recv()
        if j < 3:
            when(both(odd, up_to(j, THIRD)) if j in ACROSS else up_to(j, THIRD), go, on_down[j])
        if j == 2:
            by_core(hand_on(1, 0), go)
            by_core(hand_on(2, 0), go)
            for copy in note_out:
                copy.wait_recv()
            to_scalar = pltpu.make_async_copy(meta, smeta, smeta_sem)
            to_scalar.start()
            to_scalar.wait()
            load_own.wait()
            absorb(0, own, True)
        if j == 3:
            v_on_down.start()
            when(c == 0, go, v_far)
            v_facing.start()
            v_down.start()
        if j == 4:
            by_core(hand_on(1, 1), go)
            by_core(hand_on(2, 1), go)
    by_core(hand_on(1, 2), go)
    absorb(4, rb4, False)
    absorb(2, rb2, False)
    for j in range(3):
        when(up_to(j, THIRD), has_come, on_down[j])
    by_core(hand_on(3, 0), go)
    absorb(6, rb6, False)
    for d in (5, 7, 3, 1):
        here(d)
        absorb(d, rb[d], False)


    ones = jnp.ones((8, TILE), BF16)
    degree = jnp.zeros((8, TILE), F32)
    for s in range(SLOTS):
        tile = ((own[s].astype(F32) * power_of_two(exps[s])) * paths[s]).astype(BF16)
        motif[s] = tile
        degree = degree + lax.dot_general(ones, tile, NT, preferred_element_type=F32)
    degree = degree[0:1, :]
    root = lax.rsqrt(degree)

    def exchange(xs, ssem, rsem):
        direct = [
            remote(xs.at[0], xs.at[2 * k], ssem.at[k], rsem.at[2 * k], at_blk(q - k, c)) for k in (1, 2, 3)
        ]
        far = remote(xs.at[0], xs.at[7], ssem.at[4], rsem.at[7], cross)
        near = remote(xs.at[0], xs.at[1], ssem.at[5], rsem.at[1], sibling)
        direct[2].start()
        direct[1].start()
        direct[0].start()
        by_core([far, near], go)
        return direct

    def passing(xs, ssem, rsem, k):
        return [
            remote(xs.at[2 * k], xs.at[d], ssem.at[5 + k], rsem.at[d], sibling)
            for d in (2 * k - 1, 2 * k + 1)
        ]

    def relay(xs, ssem, rsem, direct):
        for k in (1, 2, 3):
            direct[k - 1].wait_recv()
            by_core(passing(xs, ssem, rsem, k), go)

    def rest(xs, ssem, rsem):
        for d in (1, 3, 5, 7):
            remote(xs.at[d], xs.at[d], ssem.at[0], rsem.at[d], sibling).wait_recv()

    def all_left(xs, ssem, rsem, direct):
        for copy in direct:
            copy.wait_send()
        far = remote(xs.at[0], xs.at[7], ssem.at[4], rsem.at[7], cross)
        near = remote(xs.at[0], xs.at[1], ssem.at[5], rsem.at[1], sibling)
        by_core([far, near], left_here)
        for k in (1, 2, 3):
            by_core(passing(xs, ssem, rsem, k), left_here)

    def apply_graph(xs):
        total = jnp.zeros((VEC, TILE), F32)
        for s in range(SLOTS):
            total = total + lax.dot_general(xs[offs[s]], motif[s], NT, preferred_element_type=F32)
        return total

    lane = lax.broadcasted_iota(jnp.int32, (64, 128), 1)
    row = lax.broadcasted_iota(jnp.int32, (64, 128), 0)
    left = lane < VEC
    zeros = jnp.zeros((64, 128), F32)

    def gram(i, vectors):
        both = dot32(vectors, jnp.concatenate([vectors, vectors], axis=0), NT)
        g_src[i] = jnp.where(left[:32], both[:32], both[32:]) / NODES

    def copies_b(i):
        own_half, other_half = pl.ds(c * HALF, HALF), pl.ds((1 - c) * HALF, HALF)
        copies = []
        for j in range(NX):
            copies.append(remote(g_src.at[i, other_half], gb.at[i, j], gbs.at[i, j], gbr.at[i, j], x_others[j]))
            if j < NX - 1:
                n = NX + j
                copies.append(remote(g_src.at[i, own_half], gb.at[i, n], gbs.at[i, n], gbr.at[i, n], x_mates[j]))
        return copies

    def copies_c(i):
        return [remote(gc_src.at[i], gc.at[i, j], gcs.at[i, j], gcr.at[i, j], y_mates[j]) for j in range(NY - 1)]

    def copies_d(i):
        return [remote(gd_src.at[i], gd.at[i, j], gds.at[i, j], gdr.at[i, j], z_mates[j]) for j in range(NZ - 1)]

    def copies_e(i):
        mine = pl.ds(c * HALF, HALF)
        return [remote(fin.at[i, mine], fin.at[i, mine], ges.at[i], ger.at[i], sibling)]

    def start(copies):
        for copy in copies:
            copy.start()

    def arrive(copies):
        for copy in copies:
            copy.wait_recv()

    def step_b(i):
        start(copies_b(i))

    def step_c(i):
        arrive(copies_b(i))
        gc_src[i] = g_src[i, pl.ds(c * HALF, HALF), :] + sum(gb[i, j] for j in range(1, 7)) + gb[i, 0]
        start(copies_c(i))

    def step_d(i):
        arrive(copies_c(i))
        gd_src[i] = gc_src[i] + sum(gc[i, j] for j in range(1, 7)) + gc[i, 0]
        start(copies_d(i))

    def step_e(i):
        arrive(copies_d(i))
        fin[i, pl.ds(c * HALF, HALF), :] = gd_src[i] + sum(gd[i, j] for j in range(1, 7)) + gd[i, 0]
        start(copies_e(i))

    def collect(i):
        other = pl.ds((1 - c) * HALF, HALF)
        remote(fin.at[i, other], fin.at[i, other], ges.at[i], ger.at[i], sibling).wait_recv()
        packed = fin[i]
        turned = pltpu.roll(packed, 64, 1)
        return jnp.concatenate(
            [jnp.where(left[:32], packed, turned), jnp.where(left[:32], turned, packed)], axis=0
        )

    def left_all(copies):
        for copy in copies:
            copy.wait_send()

    def tiles_have_left():
        left_all(note_out + [v_down, v_facing, v_on_down])
        for j in range(SLOTS):
            when(comes_down(j), left_here, own_down[j])
            own_facing[j].wait_send()
            if j < 3:
                when(both(odd, up_to(j, THIRD)) if j in ACROSS else up_to(j, THIRD), left_here, on_down[j])
            if j in ACROSS:
                when(both(odd, up_to(j, THIRD)), left_here, across[j])

        @pl.when(c == 0)
        def _():
            left_all([far_tile, v_far])

        @pl.when(c == 1)
        def _():
            left_all(near_tiles + [v_near])

        for core in range(2):
            @pl.when(c == core)
            def _(core=core):
                for k in (1, 2, 3):
                    for p in range(3):
                        copy = hand_on(k, p)[core]
                        if copy is not None:
                            copy.wait_send()
                    v_hand_on[k][core].wait_send()

    roots[0] = root
    root_out = [
        remote(roots.at[0], roots.at[d], rsend.at[d], rrecv.at[d], at_behind(d)) for d in (7, 6, 5, 4, 3, 2, 1)
    ]
    start(root_out)
    v_facing.wait_recv()
    by_core(v_hand_on[1], go)
    v_down.wait_recv()
    by_core(v_hand_on[2], go)
    v_on_down.wait_recv()
    by_core(v_hand_on[3], go)
    tiles_have_left()
    for d in (1, 3, 5, 7):
        vectors(0, d, 0, sibling).wait_recv()
    arrive(root_out)
    total = jnp.zeros((VEC, TILE), F32)
    for s in range(SLOTS):
        input_s = (vs[offs[s]].astype(F32) * roots[offs[s]]).astype(BF16)
        total = total + lax.dot_general(input_s, motif[s], NT, preferred_element_type=F32)
    input_1 = (vs[0].astype(F32) * root).astype(BF16).astype(F32)
    scaled_1 = (total + degree * input_1) * root

    wide_2 = scaled_1 * root
    xs2[0] = wide_2.astype(BF16)
    sent_2 = exchange(xs2, x2s, x2r)
    gram(0, scaled_1)
    step_b(0)
    relay(xs2, x2s, x2r, sent_2)
    step_c(0)
    rest(xs2, x2s, x2r)
    scaled_2 = (apply_graph(xs2) + degree * wide_2) * root
    gram(1, scaled_2)
    step_b(1)
    step_d(0)
    step_c(1)
    left_all(root_out)
    all_left(xs2, x2s, x2r, sent_2)
    left_all(copies_b(0) + copies_c(0))
    step_e(0)
    step_d(1)
    gram_1 = collect(0)
    augmented = jnp.where(left, gram_1, jnp.where(lane == row + VEC, 1.0, 0.0))
    blocks = eliminate([augmented[8 * i : 8 * i + 8] for i in range(8)], 0, VEC)
    inverse_1 = jnp.where(left, 0.0, finish(blocks))
    left_all(copies_d(0) + copies_e(0) + copies_b(1) + copies_c(1))
    step_e(1)
    left_all(copies_d(1))
    gram_2 = jnp.where(left, 0.0, collect(1))
    half_way = dot32(inverse_1, jnp.concatenate([zeros, gram_2], axis=0))
    middle = dot32(half_way, jnp.concatenate([inverse_1, zeros], axis=0), NT)
    augmented = jnp.where(left, middle, inverse_1)
    blocks = eliminate([augmented[8 * i : 8 * i + 8] for i in range(8)], 0, VEC)
    inverse_2 = jnp.where(left, 0.0, finish(blocks))
    out[...] = dot32(inverse_2, jnp.concatenate([jnp.zeros((VEC, TILE), F32), scaled_2], axis=0))
    left_all(copies_e(1))


def shards(tile_values, tile_offset, tile_exponent, initial_vectors):
    dma = pltpu.SemaphoreType.DMA
    tiles = [pltpu.VMEM((ROWS[d], TILE, TILE), BF16) for d in range(1, REACH)]
    basis_t = pl.pallas_call(
        kernel,
        out_shape=jax.ShapeDtypeStruct((VEC, TILE), F32),
        in_specs=[
            pl.BlockSpec(memory_space=pltpu.HBM),
            pl.BlockSpec(memory_space=pltpu.HBM),
            pl.BlockSpec(memory_space=pltpu.HBM),
            pl.BlockSpec(memory_space=pltpu.HBM),
        ],
        out_specs=pl.BlockSpec(memory_space=pltpu.VMEM),
        scratch_shapes=[
            pltpu.VMEM((SLOTS, TILE, TILE), BF16),
            *tiles,
            pltpu.SMEM((1, SLOTS), jnp.int32),
            pltpu.SMEM((1, SLOTS), jnp.int32),
            pltpu.VMEM((REACH, 8, 128), jnp.int32),
            pltpu.SMEM((REACH, 8, 128), jnp.int32),
            pltpu.VMEM((SLOTS, TILE, TILE), F32),
            pltpu.VMEM((SLOTS, TILE, TILE), BF16),
            pltpu.VMEM((REACH, VEC, TILE), BF16),
            pltpu.VMEM((REACH, 1, TILE), F32),
            pltpu.VMEM((REACH, VEC, TILE), BF16),
            pltpu.VMEM((2, 2 * HALF, 128), F32),
            pltpu.VMEM((2, 2 * NX - 1, HALF, 128), F32),
            pltpu.VMEM((2, HALF, 128), F32),
            pltpu.VMEM((2, NY - 1, HALF, 128), F32),
            pltpu.VMEM((2, HALF, 128), F32),
            pltpu.VMEM((2, NZ - 1, HALF, 128), F32),
            pltpu.VMEM((2, 2 * HALF, 128), F32),
            dma, dma((3,)), dma,
            dma((31,)), dma((8, 6)), dma((8, 3)),
            dma((8,)), dma((8,)),
            dma((9,)), dma((8,)),
            dma((8,)), dma((8,)),
            dma((9,)), dma((8,)),
            dma((2, 2 * NX - 1)), dma((2, 2 * NX - 1)),
            dma((2, NY - 1)), dma((2, NY - 1)),
            dma((2, NZ - 1)), dma((2, NZ - 1)),
            dma((2,)), dma((2,)),
        ],
        compiler_params=pltpu.CompilerParams(
            collective_id=0, has_side_effects=True, vmem_limit_bytes=55000 * 1024
        ),
        cost_estimate=pl.CostEstimate(flops=1200000000, bytes_accessed=1000000, transcendentals=0),
        name="embed",
    )(tile_values, tile_offset, tile_exponent, initial_vectors.T)
    return basis_t.T


def solution(mesh):
    return jax.shard_map(
        shards,
        mesh=mesh,
        in_specs=(
            P(("grp", "blk"), None, None, None),
            P(("grp", "blk"), None),
            P(("grp", "blk"), None),
            P(("grp", "blk"), None),
        ),
        out_specs=P(("grp", "blk"), None),
        check_vma=False,
    )
```
